32 devices in a mesh: fsdp: 16 (over z, y, x), rep: 2 (over core).
Axes of the slice: x: 2, y: 2, z: 4, core: 2. Of those that a mesh axis runs over, the one named last changes fastest.
Arguments:
- hidden_in: bfloat16 [2, 2048, 1024], P(None, ('fsdp', 'rep')), may hold values from -6 to 6
- seq_lengths: int32 [2, 32, 4], P(None, ('fsdp', 'rep')), may hold values from 1 to 32, 64 in all within a row
- out_grad: bfloat16 [2, 2048, 1024], P(None, ('fsdp', 'rep')), may hold values from -6 to 6
- in_gain: bfloat16 [1024], P('fsdp'), may hold values from 0.5 to 1.5
- mixer_in: bfloat16 [1024, 3352], P('fsdp'), may hold values from -0.1875 to 0.1875
- conv_weight: bfloat16 [4, 1792], P(None, 'fsdp'), may hold values from -3 to 3
- conv_bias: bfloat16 [1792], P('fsdp'), may hold values from -3 to 3
- head_params: float32 [3, 24], replicated, may hold values from -4.5 to 2
- mixer_gain: bfloat16 [1536], P('fsdp'), may hold values from 0.5 to 1.5
- mixer_out: bfloat16 [1536, 1024], P('fsdp'), may hold values from -0.15625 to 0.15625
- qkv_weight: bfloat16 [1024, 768], P('fsdp'), may hold values from -0.1875 to 0.1875
- attn_out: bfloat16 [512, 1024], P('fsdp'), may hold values from -0.75 to 0.75
- ffn_gain: bfloat16 [1024], P('fsdp'), may hold values from 0.5 to 1.5
- gate_up: bfloat16 [1024, 4096], P('fsdp'), may hold values from -0.1875 to 0.1875
- ffn_down: bfloat16 [2048, 1024], P('fsdp'), may hold values from -0.125 to 0.125
Outputs:
- hidden_out: bfloat16 [2, 2048, 1024], P(None, ('fsdp', 'rep'))
- input_grad: float32 [2, 2048, 1024], P(None, ('fsdp', 'rep'))
- in_gain_grad: float32 [1024], P('fsdp')
- mixer_in_grad: float32 [1024, 3352], P('fsdp')
- conv_weight_grad: float32 [4, 1792], P(None, 'fsdp')
- conv_bias_grad: float32 [1792], P('fsdp')
- head_params_grad: float32 [3, 24], replicated
- mixer_gain_grad: float32 [1536], P('fsdp')
- mixer_out_grad: float32 [1536, 1024], P('fsdp')
- qkv_weight_grad: float32 [1024, 768], P('fsdp')
- attn_out_grad: float32 [512, 1024], P('fsdp')
- ffn_gain_grad: float32 [1024], P('fsdp')
- gate_up_grad: float32 [1024, 4096], P('fsdp')
- ffn_down_grad: float32 [2048, 1024], P('fsdp')
The draws below stay inside these ranges and needn't reach their ends.
Inputs may be any that keep to these rules, and one draw needn't show every extreme that they name: `seq_lengths`: each device's 4 lengths in a micro-batch sum to 64; the longest is 32.
All inputs are finite; a program needn't handle non-finite values.
Results may differ from the reference program's by a relative error of at most 0.012.
Values may be sent and summed in bfloat16 or wider, within the bound.
A program may use at most 192 MiB of HBM per device.

```python
import math
import jax
import jax.numpy as jnp
import numpy as np
from jax import lax

D = 1024
HEADS = 24
HEAD_DIM = 64
STATE = 128
CONV = 4
QUERY_HEADS = 8
KEY_VALUE_HEADS = 2
HEAD_SIZE = 64
FF = 2048
TOK_DEV = 64
SEQS = 4
MICRO = 2
DSSM = 1536
XBC = 1792
MIX_IN = 3352
QKV = 768
MOST = 32
NDEV = 32
TOKENS = 2048
N_FSDP = 16
N_REP = 2


def draw_head_params(key, part):
    key = jax.random.fold_in(key, 5)
    uniform_draw = jax.random.uniform(key, (3, HEADS), jnp.float32)
    lower_end = jnp.array([-4.5, -1.0, 0.5], jnp.float32)
    upper_end = jnp.array([0.5, 2.0, 1.5], jnp.float32)
    return lower_end[:, None] + (upper_end - lower_end)[:, None] * uniform_draw


def with_spikes(entries, key, source, target, parts, factor):
    owner, partner = [(jnp.arange(entries.shape[axis_at]) // (entries.shape[axis_at] // parts)).reshape([-1 if axis == axis_at else 1 for axis in range(entries.ndim)]) for axis_at in (source, target)]
    chosen = jax.random.permutation(key, parts)[partner]
    strong = (owner == chosen) | (owner == (partner + parts // 2) % parts)
    return jnp.where(strong, factor * entries, entries)


def steps_of(key, extent, shards, least, top_value):
    gain = 1.0
    for dim, shards_of in shards:
        steps = jax.random.uniform(jax.random.fold_in(jax.random.fold_in(key, 6), dim), (shards_of,), jnp.float32, least / len(shards), top_value / len(shards))
        gain = gain * jnp.repeat(jnp.exp(steps), extent[dim] // shards_of).reshape((-1,) + (1,) * (len(extent) - 1 - dim))
    return gain


def length_profile(number_of, total, limit, slope):
    portions = [(1 << 20) // math.isqrt(rank ** slope) + 1 for rank in range(2, number_of + 1)]
    surplus, holding = total - limit - (number_of - 1), [1] * (number_of - 1)
    while surplus > 0:
        candidates = [i for i in range(number_of - 1) if holding[i] < limit]
        mass, budget = sum([portions[i] for i in candidates]), surplus
        for i in candidates:
            addition = min(limit - holding[i], max(1, budget * portions[i] // mass), surplus)
            holding[i] = holding[i] + addition
            surplus = surplus - addition
    return np.array([limit] + holding)


def uneven(key, amount, total, reach, skew):
    if amount == 2:
        one = jax.random.randint(key, (), max(1, total - reach), min(reach, total - 1) + 1)
        return jnp.stack([one, total - one])
    sizes = jnp.asarray(length_profile(amount, total, reach, skew), jnp.int32)
    twos = (amount - 1) // 2
    source_of, receiver = sizes[1:1 + 2 * twos:2], sizes[2:2 + 2 * twos:2]
    margin = jnp.minimum(source_of - 1, reach - receiver)
    moved = jax.random.randint(jax.random.fold_in(key, 1), (twos,), 0, 1 << 20) % (margin + 1)
    sizes = sizes.at[1:1 + 2 * twos:2].set(source_of - moved).at[2:2 + 2 * twos:2].set(receiver + moved)
    return sizes[jax.random.permutation(jax.random.fold_in(key, 2), amount)]


def gaussian(stream_key, shape, scale, reach, shards=(), held_as=jnp.bfloat16):
    values = scale * jax.random.normal(stream_key, shape, jnp.float32)
    if shards:
        values = values * steps_of(stream_key, shape, shards, -0.22, 0.18)
    return jnp.clip(values, -reach, reach).astype(held_as)


def bell_draw_with(own_key, dims, spread, limit, shards, heavy, held_as=jnp.bfloat16):
    values = spread * jax.random.normal(own_key, dims, jnp.float32)
    if shards:
        values = values * steps_of(own_key, dims, shards, -0.22, 0.18)
    return jnp.clip(with_spikes(values, jax.random.fold_in(own_key, 3), *heavy), -limit, limit).astype(held_as)


def setup_inputs(seed: int = 0) -> dict:
    key_list = jax.random.split(jax.random.key(seed), 16)
    hidden_in = bell_draw_with(key_list[0], (MICRO, TOKENS, D), 1.0, 6.0, ((1, 32),), (1, 2, 32, 2.75))
    seq_lengths = jax.vmap(lambda own: uneven(own, SEQS, TOK_DEV, MOST, 2))(jax.random.split(key_list[1], MICRO * NDEV)).reshape((MICRO, NDEV, SEQS)).astype(jnp.int32)
    out_grad = gaussian(key_list[2], (MICRO, TOKENS, D), 1.0, 6.0, ((1, 32),))
    in_gain = jnp.clip(1.0 + 0.1 * jax.random.normal(key_list[3], (D,), jnp.float32), 0.5, 1.5).astype(jnp.bfloat16)
    mixer_in = gaussian(key_list[4], (D, MIX_IN), D ** -0.5, 0.1875, ((0, 16),))
    conv_weight = gaussian(key_list[5], (CONV, XBC), 0.5, 3.0, ((1, 16),))
    conv_bias = gaussian(key_list[6], (XBC,), 0.5, 3.0, ((0, 16),))
    head_params = draw_head_params(jax.random.fold_in(key_list[15], 71), 0)
    mixer_gain = jnp.clip(1.0 + 0.1 * jax.random.normal(key_list[8], (DSSM,), jnp.float32), 0.5, 1.5).astype(jnp.bfloat16)
    mixer_out = gaussian(key_list[9], (DSSM, D), DSSM ** -0.5, 0.15625, ((0, 16),))
    qkv_weight = gaussian(key_list[10], (D, QKV), D ** -0.5, 0.1875, ((0, 16),))
    attn_out = gaussian(key_list[11], (QUERY_HEADS * HEAD_SIZE, D), (QUERY_HEADS * HEAD_SIZE // 8) ** -0.5, 0.75, ((0, 16),))
    ffn_gain = jnp.clip(1.0 + 0.1 * jax.random.normal(key_list[12], (D,), jnp.float32), 0.5, 1.5).astype(jnp.bfloat16)
    gate_up = gaussian(key_list[13], (D, 2 * FF), D ** -0.5, 0.1875, ((0, 16),))
    ffn_down = gaussian(key_list[14], (FF, D), FF ** -0.5, 0.125, ((0, 16),))
    return dict(hidden_in=hidden_in, seq_lengths=seq_lengths, out_grad=out_grad, in_gain=in_gain, mixer_in=mixer_in, conv_weight=conv_weight, conv_bias=conv_bias, head_params=head_params, mixer_gain=mixer_gain, mixer_out=mixer_out, qkv_weight=qkv_weight, attn_out=attn_out, ffn_gain=ffn_gain, gate_up=gate_up, ffn_down=ffn_down)


@jax.custom_vjp
def low(v):
    return lax.optimization_barrier(v.astype(jnp.bfloat16)).astype(jnp.float32)

@jax.custom_vjp
def low_back(v):
    return v

def low_keep(v):
    return (low(v), None)

def low_pass(kept, grad):
    return (grad,)

def back_keep(v):
    return (v, None)

def back_low(kept, grad):
    return (low(grad),)
low.defvjp(low_keep, low_pass)
low_back.defvjp(back_keep, back_low)
epsilon = 1e-05
highest = lax.Precision.HIGHEST
rope_base = 10000.0

def product(left, right):
    return jnp.dot(left, right, precision=highest)

def rms_scale(value_rows):
    return lax.rsqrt(lax.optimization_barrier(jnp.mean(value_rows * value_rows, axis=1, keepdims=True)) + epsilon)

def layout(lengths, count_of_tokens):
    seq_ends = jnp.cumsum(lengths, dtype=jnp.int32)
    places = jnp.arange(count_of_tokens, dtype=jnp.int32)
    passed = (places[:, None] >= seq_ends[None, :]).astype(jnp.int32)
    segment = lax.optimization_barrier(jnp.sum(passed, axis=1, dtype=jnp.int32))
    starts = lax.optimization_barrier(jnp.sum(passed * lengths[None, :], axis=1, dtype=jnp.int32))
    return (segment, places - starts)

def delayed(value_rows, segment, lag_rows):
    count_of_tokens = value_rows.shape[0]
    shifted = jnp.concatenate([jnp.zeros((lag_rows, value_rows.shape[1]), value_rows.dtype), value_rows[:count_of_tokens - lag_rows]], axis=0)
    earlier = jnp.concatenate([jnp.full((lag_rows,), -1, jnp.int32), segment[:count_of_tokens - lag_rows]], axis=0)
    return jnp.where((earlier == segment)[:, None], shifted, 0.0)

def rotary(position):
    half_width = HEAD_SIZE // 2
    inverse_freq = jnp.exp(jnp.arange(half_width, dtype=jnp.float32) * (-2.0 * math.log(rope_base) / HEAD_SIZE))
    angles = position.astype(jnp.float32)[:, None] * inverse_freq[None, :]
    cosine_table = jnp.concatenate([jnp.cos(angles), jnp.cos(angles)], axis=1)
    sine_table = jnp.concatenate([jnp.sin(angles), jnp.sin(angles)], axis=1)
    return (cosine_table, sine_table)

def rotate(value_rows):
    first_half, second_half = jnp.split(value_rows, 2, axis=-1)
    return jnp.concatenate([-second_half, first_half], axis=-1)

def block_forward(params, tokens, lengths):
    gain_one, w_mix, w_conv, b_conv, head_params, gain_mix, w_mout, w_qkv, w_att, gain_two, w_gu, w_down = params
    count_of_tokens = tokens.shape[0]
    segment, position = layout(lengths, count_of_tokens)
    places = jnp.arange(count_of_tokens, dtype=jnp.int32)
    visible = (segment[:, None] == segment[None, :]) & (places[:, None] >= places[None, :])
    normed = low(tokens * rms_scale(tokens) * gain_one[None, :])
    projected = low_back(product(normed, w_mix))
    gate_z = projected[:, :DSSM]
    conv_input = projected[:, DSSM:DSSM + XBC]
    step_raw = projected[:, DSSM + XBC:]
    conv_sum = jnp.broadcast_to(b_conv[None, :], (count_of_tokens, XBC))
    for offset in range(CONV):
        conv_sum = conv_sum + w_conv[offset][None, :] * delayed(conv_input, segment, CONV - 1 - offset)
    conv_out = jax.nn.silu(conv_sum)
    inner_x = conv_out[:, :DSSM].reshape(count_of_tokens, HEADS, HEAD_DIM)
    input_b = conv_out[:, DSSM:DSSM + STATE]
    input_c = conv_out[:, DSSM + STATE:]
    step_size = jax.nn.softplus(step_raw + head_params[0][None, :])
    decay_rate = -jnp.exp(head_params[1])
    cumulative = jnp.cumsum(step_size * decay_rate[None, :], axis=0)
    inside = visible[:, :, None]
    decay_mask = jnp.where(inside, jnp.exp(jnp.where(inside, cumulative[:, None, :] - cumulative[None, :, :], 0.0)), 0.0)
    intersection = product(input_c, input_b.T)
    mixing = intersection[:, :, None] * decay_mask
    scaled_in = inner_x * step_size[:, :, None]
    ssd_out = jnp.einsum('tsh,shp->thp', mixing, scaled_in, precision=highest) + head_params[2][None, :, None] * inner_x
    gated_out = ssd_out.reshape(count_of_tokens, DSSM) * jax.nn.silu(gate_z)
    mixed_low = low(gated_out * rms_scale(gated_out) * gain_mix[None, :])
    mixer_branch = low_back(product(mixed_low, w_mout))
    query_key_value_output = low_back(product(normed, w_qkv))
    query_group_width = QUERY_HEADS // KEY_VALUE_HEADS
    query_rows = query_key_value_output[:, :QUERY_HEADS * HEAD_SIZE].reshape(count_of_tokens, KEY_VALUE_HEADS, query_group_width, HEAD_SIZE)
    key_matrix_rows = query_key_value_output[:, QUERY_HEADS * HEAD_SIZE:(QUERY_HEADS + KEY_VALUE_HEADS) * HEAD_SIZE].reshape(count_of_tokens, KEY_VALUE_HEADS, HEAD_SIZE)
    value_rows = query_key_value_output[:, (QUERY_HEADS + KEY_VALUE_HEADS) * HEAD_SIZE:].reshape(count_of_tokens, KEY_VALUE_HEADS, HEAD_SIZE)
    cosine_table, sine_table = rotary(position)
    rot_q = low(query_rows * cosine_table[:, None, None, :] + rotate(query_rows) * sine_table[:, None, None, :])
    rot_k = low(key_matrix_rows * cosine_table[:, None, :] + rotate(key_matrix_rows) * sine_table[:, None, :])
    value_low = low(value_rows)
    scores = low_back(jnp.einsum('tkgd,skd->kgts', rot_q, rot_k, precision=highest) * HEAD_SIZE ** (-0.5))
    scores = jnp.where(visible[None, None], scores, -1e+30)
    exponent = jnp.exp(scores - lax.optimization_barrier(jnp.max(scores, axis=3, keepdims=True)))
    attention_probs = exponent / lax.optimization_barrier(jnp.sum(exponent, axis=3, keepdims=True))
    attended = low(low_back(jnp.einsum('kgts,skd->tkgd', low(attention_probs), value_low, precision=highest)))
    attn_branch = low_back(product(attended.reshape(count_of_tokens, QUERY_HEADS * HEAD_SIZE), w_att))
    residual = tokens + mixer_branch + attn_branch
    normed_two = low(residual * rms_scale(residual) * gain_two[None, :])
    gate_upv = low_back(product(normed_two, w_gu))
    activated = low(jax.nn.silu(gate_upv[:, :FF]) * gate_upv[:, FF:])
    ffn_branch = low_back(product(activated, w_down))
    return residual + ffn_branch

def reference(hidden_in, seq_lengths, out_grad, in_gain, mixer_in, conv_weight, conv_bias, head_params, mixer_gain, mixer_out, qkv_weight, attn_out, ffn_gain, gate_up, ffn_down):
    params = (in_gain.astype(jnp.float32), mixer_in.astype(jnp.float32), conv_weight.astype(jnp.float32), conv_bias.astype(jnp.float32), head_params.astype(jnp.float32), mixer_gain.astype(jnp.float32), mixer_out.astype(jnp.float32), qkv_weight.astype(jnp.float32), attn_out.astype(jnp.float32), ffn_gain.astype(jnp.float32), gate_up.astype(jnp.float32), ffn_down.astype(jnp.float32))
    blocks = MICRO * N_FSDP * N_REP
    group_blocks = math.gcd(blocks, 16)
    step_count = blocks // group_blocks
    tokens = hidden_in.astype(jnp.float32).reshape(blocks, TOK_DEV, D)
    lengths = seq_lengths.reshape(blocks, SEQS)
    cotangent = out_grad.astype(jnp.float32).reshape(blocks, TOK_DEV, D)

    def forward(params, tokens):

        def one_step(carried, inputs):
            token_group, length_group = inputs

            def single(token_block, length_block):
                return block_forward(params, token_block, length_block)
            return (carried, jax.vmap(single)(token_group, length_group))
        checkpointed = jax.checkpoint(one_step)
        _, results = lax.scan(checkpointed, jnp.zeros((), jnp.float32), (tokens.reshape(step_count, group_blocks, TOK_DEV, D), lengths.reshape(step_count, group_blocks, SEQS)))
        return results.reshape(blocks, TOK_DEV, D)
    result, pullback = jax.vjp(forward, params, tokens)
    param_grads, token_grad = pullback(cotangent)
    hidden_out = result.reshape(MICRO, N_FSDP * N_REP * TOK_DEV, D).astype(jnp.bfloat16)
    input_grad = token_grad.reshape(MICRO, N_FSDP * N_REP * TOK_DEV, D)
    return (hidden_out, input_grad, param_grads[0], param_grads[1], param_grads[2], param_grads[3], param_grads[4], param_grads[5], param_grads[6], param_grads[7], param_grads[8], param_grads[9], param_grads[10], param_grads[11])
```

```python
import functools
import math

import jax
import jax.numpy as jnp
from jax import lax
from jax.experimental import pallas as pl
from jax.experimental.pallas import tpu as pltpu
from jax.sharding import PartitionSpec as P

HEADS = 24
HEAD_DIM = 64
STATE = 128
CONV = 4
QUERY_HEADS = 8
KEY_VALUE_HEADS = 2
HEAD_SIZE = 64
FF = 2048
MICRO = 2
DSSM = 1536
XBC = 1792


epsilon = 1e-05
highest = lax.Precision.HIGHEST
rope_base = 10000.0


def dot_bf(left, right):
    return jnp.dot(left, right, preferred_element_type=jnp.float32)


def dot_left(left, right):
    return lax.dot_general(
        left, right, (((0,), (0,)), ((), ())), preferred_element_type=jnp.float32
    )


def dot_right(left, right):
    return lax.dot_general(
        left, right, (((1,), (1,)), ((), ())), preferred_element_type=jnp.float32
    )


def rms_scale(value_rows):
    return lax.rsqrt(jnp.mean(value_rows * value_rows, axis=1, keepdims=True) + epsilon)


def norm_back(grad_normed, value_rows, scale_rows, gain_row):
    weighted = grad_normed * gain_row[None, :]
    inner_mean = jnp.mean(weighted * value_rows, axis=1, keepdims=True)
    return scale_rows * weighted - value_rows * scale_rows * scale_rows * scale_rows * inner_mean


def silu_slope(value_rows):
    sigma_v = jax.nn.sigmoid(value_rows)
    return sigma_v * (1.0 + value_rows * (1.0 - sigma_v))


def layout(lengths, count_of_tokens):
    seq_ends = jnp.cumsum(lengths, dtype=jnp.int32)
    places = jnp.arange(count_of_tokens, dtype=jnp.int32)
    passed = (places[:, None] >= seq_ends[None, :]).astype(jnp.int32)
    segment = jnp.sum(passed, axis=1, dtype=jnp.int32)
    starts = jnp.sum(passed * lengths[None, :], axis=1, dtype=jnp.int32)
    return (segment, places - starts)


def delay_keep(segment, lag_rows):
    count_of_tokens = segment.shape[0]
    earlier = jnp.concatenate(
        [jnp.full((lag_rows,), -1, jnp.int32), segment[: count_of_tokens - lag_rows]], axis=0
    )
    return earlier == segment


def delayed(value_rows, segment, lag_rows):
    count_of_tokens = value_rows.shape[0]
    shifted = jnp.concatenate(
        [
            jnp.zeros((lag_rows, value_rows.shape[1]), value_rows.dtype),
            value_rows[: count_of_tokens - lag_rows],
        ],
        axis=0,
    )
    return jnp.where(delay_keep(segment, lag_rows)[:, None], shifted, 0.0)


def rotary(position):
    half_width = HEAD_SIZE // 2
    inverse_freq = jnp.exp(
        jnp.arange(half_width, dtype=jnp.float32) * (-2.0 * math.log(rope_base) / HEAD_SIZE)
    )
    angles = position.astype(jnp.float32)[:, None] * inverse_freq[None, :]
    cosine_table = jnp.concatenate([jnp.cos(angles), jnp.cos(angles)], axis=1)
    sine_table = jnp.concatenate([jnp.sin(angles), jnp.sin(angles)], axis=1)
    return (cosine_table, sine_table)


def rotate(value_rows):
    first_half, second_half = jnp.split(value_rows, 2, axis=-1)
    return jnp.concatenate([-second_half, first_half], axis=-1)


def rotate_back(value_rows):
    first_half, second_half = jnp.split(value_rows, 2, axis=-1)
    return jnp.concatenate([second_half, -first_half], axis=-1)


def collect(
    in_gain,
    mixer_in,
    conv_weight,
    conv_bias,
    mixer_gain,
    mixer_out,
    qkv_weight,
    attn_out,
    ffn_gain,
    gate_up,
    ffn_down,
):
    return (
        lax.all_gather(in_gain, "fsdp", axis=0, tiled=True),
        lax.all_gather(mixer_in, "fsdp", axis=0, tiled=True),
        lax.all_gather(conv_weight, "fsdp", axis=1, tiled=True),
        lax.all_gather(conv_bias, "fsdp", axis=0, tiled=True),
        lax.all_gather(mixer_gain, "fsdp", axis=0, tiled=True),
        lax.all_gather(mixer_out, "fsdp", axis=0, tiled=True),
        lax.all_gather(qkv_weight, "fsdp", axis=0, tiled=True),
        lax.all_gather(attn_out, "fsdp", axis=0, tiled=True),
        lax.all_gather(ffn_gain, "fsdp", axis=0, tiled=True),
        lax.all_gather(gate_up, "fsdp", axis=0, tiled=True),
        lax.all_gather(ffn_down, "fsdp", axis=0, tiled=True),
    )


def micro_step(tokens, lengths, cotangent, gathered, head_params):
    (
        in_gain,
        mixer_in,
        conv_weight,
        conv_bias,
        mixer_gain,
        mixer_out,
        qkv_weight,
        attn_out,
        ffn_gain,
        gate_up,
        ffn_down,
    ) = gathered
    count_of_tokens = tokens.shape[0]
    x_float = tokens.astype(jnp.float32)
    segment, position = layout(lengths, count_of_tokens)
    places = jnp.arange(count_of_tokens, dtype=jnp.int32)
    visible = (segment[:, None] == segment[None, :]) & (places[:, None] >= places[None, :])
    gain_one = in_gain.astype(jnp.float32)
    scale_one = rms_scale(x_float)
    normed = (x_float * scale_one * gain_one[None, :]).astype(jnp.bfloat16)
    projected = dot_bf(normed, mixer_in)
    gate_z = projected[:, :DSSM]
    conv_input = projected[:, DSSM : DSSM + XBC]
    step_raw = projected[:, DSSM + XBC :]
    conv_taps = conv_weight.astype(jnp.float32)
    conv_sum = jnp.broadcast_to(conv_bias.astype(jnp.float32)[None, :], (count_of_tokens, XBC))
    tap_inputs = []
    for offset in range(CONV):
        tap_value = delayed(conv_input, segment, CONV - 1 - offset)
        tap_inputs.append(tap_value)
        conv_sum = conv_sum + conv_taps[offset][None, :] * tap_value
    conv_out = jax.nn.silu(conv_sum)
    inner_x = conv_out[:, :DSSM].reshape(count_of_tokens, HEADS, HEAD_DIM)
    input_b = conv_out[:, DSSM : DSSM + STATE]
    input_c = conv_out[:, DSSM + STATE :]
    step_in = step_raw + head_params[0][None, :]
    step_size = jax.nn.softplus(step_in)
    decay_rate = -jnp.exp(head_params[1])
    skip_factor = head_params[2]
    cumulative = jnp.cumsum(step_size * decay_rate[None, :], axis=0)
    inside = visible[:, :, None]
    decay_mask = jnp.where(
        inside,
        jnp.exp(jnp.where(inside, cumulative[:, None, :] - cumulative[None, :, :], 0.0)),
        0.0,
    )
    intersection = jnp.dot(input_c, input_b.T, precision=highest)
    mixing = intersection[:, :, None] * decay_mask
    scaled_in = inner_x * step_size[:, :, None]
    ssd_out = (
        jnp.einsum("tsh,shp->thp", mixing, scaled_in, precision=highest)
        + skip_factor[None, :, None] * inner_x
    )
    flat_ssd = ssd_out.reshape(count_of_tokens, DSSM)
    silu_z = jax.nn.silu(gate_z)
    gated_out = flat_ssd * silu_z
    gain_mix = mixer_gain.astype(jnp.float32)
    scale_two = rms_scale(gated_out)
    mixed_low = (gated_out * scale_two * gain_mix[None, :]).astype(jnp.bfloat16)
    mixer_branch = dot_bf(mixed_low, mixer_out)
    query_key_value_output = dot_bf(normed, qkv_weight)
    query_group_width = QUERY_HEADS // KEY_VALUE_HEADS
    query_rows = query_key_value_output[:, : QUERY_HEADS * HEAD_SIZE].reshape(
        count_of_tokens, KEY_VALUE_HEADS, query_group_width, HEAD_SIZE
    )
    key_matrix_rows = query_key_value_output[
        :, QUERY_HEADS * HEAD_SIZE : (QUERY_HEADS + KEY_VALUE_HEADS) * HEAD_SIZE
    ].reshape(count_of_tokens, KEY_VALUE_HEADS, HEAD_SIZE)
    value_rows = query_key_value_output[:, (QUERY_HEADS + KEY_VALUE_HEADS) * HEAD_SIZE :].reshape(
        count_of_tokens, KEY_VALUE_HEADS, HEAD_SIZE
    )
    cosine_table, sine_table = rotary(position)
    rot_q = (
        query_rows * cosine_table[:, None, None, :]
        + rotate(query_rows) * sine_table[:, None, None, :]
    ).astype(jnp.bfloat16)
    rot_k = (
        key_matrix_rows * cosine_table[:, None, :]
        + rotate(key_matrix_rows) * sine_table[:, None, :]
    ).astype(jnp.bfloat16)
    value_low = value_rows.astype(jnp.bfloat16)
    score_scale = HEAD_SIZE ** (-0.5)
    scores = (
        jnp.einsum("tkgd,skd->kgts", rot_q, rot_k, preferred_element_type=jnp.float32) * score_scale
    )
    scores = jnp.where(visible[None, None], scores, -1e30)
    exponent = jnp.exp(scores - jnp.max(scores, axis=3, keepdims=True))
    attention_probs = exponent / jnp.sum(exponent, axis=3, keepdims=True)
    probs_low = attention_probs.astype(jnp.bfloat16)
    attended = jnp.einsum(
        "kgts,skd->tkgd", probs_low, value_low, preferred_element_type=jnp.float32
    )
    attended = attended.reshape(count_of_tokens, QUERY_HEADS * HEAD_SIZE).astype(jnp.bfloat16)
    attn_branch = dot_bf(attended, attn_out)
    residual = x_float + mixer_branch + attn_branch
    gain_two = ffn_gain.astype(jnp.float32)
    scale_three = rms_scale(residual)
    normed_two = (residual * scale_three * gain_two[None, :]).astype(jnp.bfloat16)
    gate_upv = dot_bf(normed_two, gate_up)
    gate_part = gate_upv[:, :FF]
    up_part = gate_upv[:, FF:]
    activated = (jax.nn.silu(gate_part) * up_part).astype(jnp.bfloat16)
    ffn_branch = dot_bf(activated, ffn_down)
    output = (residual + ffn_branch).astype(jnp.bfloat16)
    grad_out = cotangent.astype(jnp.float32)
    grad_act = dot_right(cotangent, ffn_down)
    grad_gu = jnp.concatenate(
        [grad_act * up_part * silu_slope(gate_part), grad_act * jax.nn.silu(gate_part)], axis=1
    ).astype(jnp.bfloat16)
    grad_n_two = dot_right(grad_gu, gate_up)
    grad_gain_two = jnp.sum(grad_n_two * residual * scale_three, axis=0)
    grad_residual = grad_out + norm_back(grad_n_two, residual, scale_three, gain_two)
    grad_res_low = grad_residual.astype(jnp.bfloat16)
    grad_att = (
        dot_right(grad_res_low, attn_out)
        .astype(jnp.bfloat16)
        .reshape(count_of_tokens, KEY_VALUE_HEADS, query_group_width, HEAD_SIZE)
    )
    value_gradient = jnp.einsum(
        "kgts,tkgd->skd", probs_low, grad_att, preferred_element_type=jnp.float32
    )
    grad_probs = jnp.einsum(
        "tkgd,skd->kgts", grad_att, value_low, preferred_element_type=jnp.float32
    )
    grad_scores = attention_probs * (
        grad_probs - jnp.sum(grad_probs * attention_probs, axis=3, keepdims=True)
    )
    grad_scores_low = grad_scores.astype(jnp.bfloat16)
    grad_rot_q = (
        jnp.einsum("kgts,skd->tkgd", grad_scores_low, rot_k, preferred_element_type=jnp.float32)
        * score_scale
    )
    grad_rot_k = (
        jnp.einsum("kgts,tkgd->skd", grad_scores_low, rot_q, preferred_element_type=jnp.float32)
        * score_scale
    )
    grad_q = grad_rot_q * cosine_table[:, None, None, :] + rotate_back(
        grad_rot_q * sine_table[:, None, None, :]
    )
    key_gradient = grad_rot_k * cosine_table[:, None, :] + rotate_back(
        grad_rot_k * sine_table[:, None, :]
    )
    grad_qkv = jnp.concatenate(
        [
            grad_q.reshape(count_of_tokens, QUERY_HEADS * HEAD_SIZE),
            key_gradient.reshape(count_of_tokens, KEY_VALUE_HEADS * HEAD_SIZE),
            value_gradient.reshape(count_of_tokens, KEY_VALUE_HEADS * HEAD_SIZE),
        ],
        axis=1,
    ).astype(jnp.bfloat16)
    grad_mixed = dot_right(grad_res_low, mixer_out)
    grad_gain_mix = jnp.sum(grad_mixed * gated_out * scale_two, axis=0)
    grad_gated = norm_back(grad_mixed, gated_out, scale_two, gain_mix)
    grad_ssd = (grad_gated * silu_z).reshape(count_of_tokens, HEADS, HEAD_DIM)
    grad_z = grad_gated * flat_ssd * silu_slope(gate_z)
    grad_skip = jnp.sum(grad_ssd * inner_x, axis=(0, 2))
    grad_scaled = jnp.einsum("tsh,thp->shp", mixing, grad_ssd, precision=highest)
    grad_mixing = jnp.einsum("thp,shp->tsh", grad_ssd, scaled_in, precision=highest)
    grad_intersection = jnp.sum(grad_mixing * decay_mask, axis=2)
    grad_differ = grad_mixing * mixing
    grad_cumul = jnp.sum(grad_differ, axis=1) - jnp.sum(grad_differ, axis=0)
    grad_logs = jnp.cumsum(grad_cumul[::-1], axis=0)[::-1]
    grad_delta = grad_logs * decay_rate[None, :] + jnp.sum(grad_scaled * inner_x, axis=2)
    grad_rate_log = jnp.sum(grad_logs * step_size, axis=0) * decay_rate
    grad_inner = grad_scaled * step_size[:, :, None] + skip_factor[None, :, None] * grad_ssd
    grad_step = grad_delta * jax.nn.sigmoid(step_in)
    grad_head = jnp.stack([jnp.sum(grad_step, axis=0), grad_rate_log, grad_skip], axis=0)
    grad_c = jnp.dot(grad_intersection, input_b, precision=highest)
    grad_b = jnp.dot(grad_intersection.T, input_c, precision=highest)
    grad_conv_out = jnp.concatenate(
        [grad_inner.reshape(count_of_tokens, DSSM), grad_b, grad_c], axis=1
    )
    grad_conv_sum = grad_conv_out * silu_slope(conv_sum)
    grad_conv_bias = jnp.sum(grad_conv_sum, axis=0)
    grad_conv_weight = jnp.stack(
        [jnp.sum(grad_conv_sum * tap_inputs[offset], axis=0) for offset in range(CONV)], axis=0
    )
    grad_conv_in = jnp.zeros((count_of_tokens, XBC), jnp.float32)
    for offset in range(CONV):
        lag_rows = CONV - 1 - offset
        tap_term = jnp.where(
            delay_keep(segment, lag_rows)[:, None], grad_conv_sum * conv_taps[offset][None, :], 0.0
        )
        grad_conv_in = grad_conv_in + jnp.concatenate(
            [tap_term[lag_rows:], jnp.zeros((lag_rows, XBC), jnp.float32)], axis=0
        )
    grad_proj = jnp.concatenate([grad_z, grad_conv_in, grad_step], axis=1).astype(jnp.bfloat16)
    grad_normed = dot_right(grad_proj, mixer_in) + dot_right(grad_qkv, qkv_weight)
    grad_gain_one = jnp.sum(grad_normed * x_float * scale_one, axis=0)
    grad_input = grad_residual + norm_back(grad_normed, x_float, scale_one, gain_one)
    pairs = (
        (normed, grad_proj),
        (mixed_low, grad_res_low),
        (normed, grad_qkv),
        (attended, grad_res_low),
        (normed_two, grad_gu),
        (activated, cotangent),
    )
    smalls = (
        grad_gain_one,
        grad_conv_weight,
        grad_conv_bias,
        grad_gain_mix,
        grad_gain_two,
        grad_head,
    )
    return (output, grad_input, pairs, smalls)


def on_device_any(
    hidden_in,
    seq_lengths,
    out_grad,
    in_gain,
    mixer_in,
    conv_weight,
    conv_bias,
    head_params,
    mixer_gain,
    mixer_out,
    qkv_weight,
    attn_out,
    ffn_gain,
    gate_up,
    ffn_down,
):
    gathered = None
    gathered = collect(
        in_gain,
        mixer_in,
        conv_weight,
        conv_bias,
        mixer_gain,
        mixer_out,
        qkv_weight,
        attn_out,
        ffn_gain,
        gate_up,
        ffn_down,
    )
    outputs = []
    input_grads = []
    kept_rows = []
    small_total = None
    for micro_index in range(MICRO):
        output, grad_input, pairs, smalls = micro_step(
            hidden_in[micro_index],
            seq_lengths[micro_index, 0],
            out_grad[micro_index],
            gathered,
            head_params,
        )
        outputs.append(output)
        input_grads.append(grad_input)
        kept_rows.append(pairs)
        small_total = smalls if small_total is None else jax.tree.map(jnp.add, small_total, smalls)
    full_grads = []
    for pair_index in range(6):
        left_rows = jnp.concatenate(
            [kept_rows[micro_index][pair_index][0] for micro_index in range(MICRO)], axis=0
        )
        right_rows = jnp.concatenate(
            [kept_rows[micro_index][pair_index][1] for micro_index in range(MICRO)], axis=0
        )
        full_grads.append(dot_left(left_rows, right_rows))
    grad_gain_one, grad_conv_weight, grad_conv_bias, grad_gain_mix, grad_gain_two, grad_head = (
        small_total
    )
    grad_terms = (
        grad_gain_one,
        full_grads[0],
        grad_conv_weight,
        grad_conv_bias,
        grad_gain_mix,
        full_grads[1],
        full_grads[2],
        full_grads[3],
        grad_gain_two,
        full_grads[4],
        full_grads[5],
    )
    shard_grads = (
        lax.psum_scatter(grad_terms[0], "fsdp", scatter_dimension=0, tiled=True),
        lax.psum_scatter(grad_terms[1], "fsdp", scatter_dimension=0, tiled=True),
        lax.psum_scatter(grad_terms[2], "fsdp", scatter_dimension=1, tiled=True),
        lax.psum_scatter(grad_terms[3], "fsdp", scatter_dimension=0, tiled=True),
        lax.psum_scatter(grad_terms[4], "fsdp", scatter_dimension=0, tiled=True),
        lax.psum_scatter(grad_terms[5], "fsdp", scatter_dimension=0, tiled=True),
        lax.psum_scatter(grad_terms[6], "fsdp", scatter_dimension=0, tiled=True),
        lax.psum_scatter(grad_terms[7], "fsdp", scatter_dimension=0, tiled=True),
        lax.psum_scatter(grad_terms[8], "fsdp", scatter_dimension=0, tiled=True),
        lax.psum_scatter(grad_terms[9], "fsdp", scatter_dimension=0, tiled=True),
        lax.psum_scatter(grad_terms[10], "fsdp", scatter_dimension=0, tiled=True),
    )
    halves = (
        lax.psum_scatter(
            shard_grads[0].astype(jnp.bfloat16), "rep", scatter_dimension=0, tiled=True
        ).astype(jnp.float32),
        lax.psum_scatter(
            shard_grads[1].astype(jnp.bfloat16), "rep", scatter_dimension=0, tiled=True
        ).astype(jnp.float32),
        lax.psum_scatter(
            shard_grads[2].astype(jnp.bfloat16), "rep", scatter_dimension=1, tiled=True
        ).astype(jnp.float32),
        lax.psum_scatter(
            shard_grads[3].astype(jnp.bfloat16), "rep", scatter_dimension=0, tiled=True
        ).astype(jnp.float32),
        lax.psum_scatter(
            shard_grads[4].astype(jnp.bfloat16), "rep", scatter_dimension=0, tiled=True
        ).astype(jnp.float32),
        lax.psum_scatter(
            shard_grads[5].astype(jnp.bfloat16), "rep", scatter_dimension=0, tiled=True
        ).astype(jnp.float32),
        lax.psum_scatter(
            shard_grads[6].astype(jnp.bfloat16), "rep", scatter_dimension=0, tiled=True
        ).astype(jnp.float32),
        lax.psum_scatter(
            shard_grads[7].astype(jnp.bfloat16), "rep", scatter_dimension=0, tiled=True
        ).astype(jnp.float32),
        lax.psum_scatter(
            shard_grads[8].astype(jnp.bfloat16), "rep", scatter_dimension=0, tiled=True
        ).astype(jnp.float32),
        lax.psum_scatter(
            shard_grads[9].astype(jnp.bfloat16), "rep", scatter_dimension=0, tiled=True
        ).astype(jnp.float32),
        lax.psum_scatter(
            shard_grads[10].astype(jnp.bfloat16), "rep", scatter_dimension=0, tiled=True
        ).astype(jnp.float32),
    )
    head_total = lax.psum(grad_head, ("fsdp", "rep"))
    summed = (
        lax.all_gather(halves[0].astype(jnp.bfloat16), "rep", axis=0, tiled=True).astype(
            jnp.float32
        ),
        lax.all_gather(halves[1].astype(jnp.bfloat16), "rep", axis=0, tiled=True).astype(
            jnp.float32
        ),
        lax.all_gather(halves[2].astype(jnp.bfloat16), "rep", axis=1, tiled=True).astype(
            jnp.float32
        ),
        lax.all_gather(halves[3].astype(jnp.bfloat16), "rep", axis=0, tiled=True).astype(
            jnp.float32
        ),
        lax.all_gather(halves[4].astype(jnp.bfloat16), "rep", axis=0, tiled=True).astype(
            jnp.float32
        ),
        lax.all_gather(halves[5].astype(jnp.bfloat16), "rep", axis=0, tiled=True).astype(
            jnp.float32
        ),
        lax.all_gather(halves[6].astype(jnp.bfloat16), "rep", axis=0, tiled=True).astype(
            jnp.float32
        ),
        lax.all_gather(halves[7].astype(jnp.bfloat16), "rep", axis=0, tiled=True).astype(
            jnp.float32
        ),
        lax.all_gather(halves[8].astype(jnp.bfloat16), "rep", axis=0, tiled=True).astype(
            jnp.float32
        ),
        lax.all_gather(halves[9].astype(jnp.bfloat16), "rep", axis=0, tiled=True).astype(
            jnp.float32
        ),
        lax.all_gather(halves[10].astype(jnp.bfloat16), "rep", axis=0, tiled=True).astype(
            jnp.float32
        ),
    )
    hidden_out = jnp.stack(outputs, axis=0)
    input_grad = jnp.stack(input_grads, axis=0)
    return (
        hidden_out,
        input_grad,
        summed[0],
        summed[1],
        summed[2],
        summed[3],
        head_total,
        summed[4],
        summed[5],
        summed[6],
        summed[7],
        summed[8],
        summed[9],
        summed[10],
    )


MESH = pl.DeviceIdType.MESH
NZ, NY, NX = 4, 2, 2
GRID = NZ * NY * NX


def positions():
    chip = lax.axis_index("fsdp")
    core = lax.axis_index("rep")
    z = chip // (NY * NX)
    y = (chip // NX) % NY
    x = chip % NX
    y1 = (y + core) % 2
    x1 = (x + 1 - core) % 2
    y2 = (y + 1 - core) % 2
    x2 = (x + core) % 2
    return z, y, x, y1, x1, y2, x2, core


def chip_of(z, y, x):
    return (z * NY + y) * NX + x


def greet(z, y, x, y1, x1, y2, x2, core):
    barrier = pltpu.get_barrier_semaphore()
    partners = [(chip_of((z + dz) % NZ, y, x), core) for dz in range(1, NZ)]
    partners += [(chip_of(z, y1, x1), core), (chip_of(z, y2, x2), core)]
    partners += [(chip_of(z, y, x), 1 - core)]
    for partner in partners:
        pl.semaphore_signal(barrier, inc=1, device_id=partner, device_id_type=MESH)
    pl.semaphore_wait(barrier, len(partners))


def push(src_ref, dst_ref, send_sem, recv_sem, partner):
    return pltpu.make_async_remote_copy(
        src_ref=src_ref,
        dst_ref=dst_ref,
        send_sem=send_sem,
        recv_sem=recv_sem,
        device_id=partner,
        device_id_type=MESH,
    )


def gather_kernel(count, *refs):
    shards = refs[:count]
    wholes = refs[count : 2 * count]
    own_sem, send_sem, recv_sem = refs[2 * count :]
    z, y, x, y1, x1, y2, x2, core = positions()
    greet(z, y, x, y1, x1, y2, x2, core)
    to_first = (chip_of(z, y1, x1), core)
    to_second = (chip_of(z, y2, x2), core)
    to_other = (chip_of(z, y, x), 1 - core)
    plan = []
    for w in range(count):
        half = shards[w].shape[0] // 2
        rows = pl.ds(pl.multiple_of(core * half, half), half)
        whole = wholes[w]
        own = pltpu.make_async_copy(shards[w].at[rows], whole.at[z, y, x, rows], own_sem.at[w])
        along_z = [
            push(
                shards[w].at[rows],
                whole.at[z, y, x, rows],
                send_sem.at[w, dz - 1],
                recv_sem.at[w, dz - 1],
                (chip_of((z + dz) % NZ, y, x), core),
            )
            for dz in range(1, NZ)
        ]
        column = whole.at[:, y, x, rows]
        column_first = whole.at[:, y1, x1, rows]
        along_first = push(column, column, send_sem.at[w, 3], recv_sem.at[w, 3], to_first)
        second_a = push(column, column, send_sem.at[w, 4], recv_sem.at[w, 4], to_second)
        second_b = push(column_first, column_first, send_sem.at[w, 5], recv_sem.at[w, 5], to_second)
        half_all = whole.at[:, :, :, rows]
        across = push(half_all, half_all, send_sem.at[w, 6], recv_sem.at[w, 6], to_other)
        plan.append((own, along_z, along_first, second_a, second_b, across))
    for own, along_z, _, _, _, _ in plan:
        own.start()
        for copy in along_z:
            copy.start()
    for step in range(count + 2):
        if step < count:
            own, along_z, along_first, second_a, _, _ = plan[step]
            own.wait()
            for copy in along_z:
                copy.wait_recv()
            along_first.start()
            second_a.start()
        if 1 <= step <= count:
            _, _, along_first, _, second_b, _ = plan[step - 1]
            along_first.wait_recv()
            second_b.start()
        if step >= 2:
            _, _, _, second_a, second_b, across = plan[step - 2]
            second_a.wait_recv()
            second_b.wait_recv()
            across.start()
    for _, along_z, along_first, second_a, second_b, across in plan:
        for copy in along_z:
            copy.wait_send()
        along_first.wait_send()
        second_a.wait_send()
        second_b.wait_send()
        across.wait()


def gather_all(shards):
    count = len(shards)
    gathered = pl.pallas_call(
        functools.partial(gather_kernel, count),
        out_shape=[
            jax.ShapeDtypeStruct((NZ, NY, NX) + shard.shape, shard.dtype) for shard in shards
        ],
        in_specs=[pl.BlockSpec(memory_space=pl.ANY)] * count,
        out_specs=[pl.BlockSpec(memory_space=pl.ANY)] * count,
        scratch_shapes=[
            pltpu.SemaphoreType.DMA((count,)),
            pltpu.SemaphoreType.DMA((count, 7)),
            pltpu.SemaphoreType.DMA((count, 7)),
        ],
        compiler_params=pltpu.CompilerParams(collective_id=0, has_side_effects=True),
        name="gather_weights",
    )(*shards)
    return [
        whole.reshape((GRID * shard.shape[0],) + shard.shape[1:])
        for whole, shard in zip(gathered, shards)
    ]


def scatter_kernel(count, *refs):
    head_ref = refs[0]
    parts = refs[1 : 1 + count]
    head_out = refs[1 + count]
    outs = refs[2 + count : 2 + 2 * count]
    rest = refs[2 + 2 * count :]
    held = rest[:count]
    got_second = rest[count : 2 * count]
    got_first = rest[2 * count : 3 * count]
    got_z = rest[3 * count : 4 * count]
    total = rest[4 * count : 5 * count]
    heads, load_sem, send_sem, recv_sem, head_send, head_recv = rest[5 * count :]
    z, y, x, y1, x1, y2, x2, core = positions()
    y3, x3 = 1 - y, 1 - x
    greet(z, y, x, y1, x1, y2, x2, core)
    to_first = (chip_of(z, y1, x1), core)
    to_second = (chip_of(z, y2, x2), core)
    to_other = (chip_of(z, y, x), 1 - core)
    z_peers = [((z + dz) % NZ, (chip_of((z + dz) % NZ, y, x), core)) for dz in range(1, NZ)]

    head_z = [
        push(head_ref, heads.at[z, y, x], head_send.at[k], head_recv.at[k], z_peers[k][1])
        for k in range(NZ - 1)
    ]
    for copy in head_z:
        copy.start()
    heads[z, y, x] = head_ref[...]

    plan = []
    for w in range(count):
        far_b = push(
            parts[w].at[:, y3, x3], got_second[w].at[1], send_sem.at[w, 1], recv_sem.at[w, 1], to_second
        )
        far_a = push(
            parts[w].at[:, y2, x2], got_second[w].at[0], send_sem.at[w, 0], recv_sem.at[w, 0], to_second
        )
        near = push(held[w].at[1], got_first[w], send_sem.at[w, 2], recv_sem.at[w, 2], to_first)
        along_z = [
            push(
                held[w].at[0, z_peers[k][0]],
                got_z[w].at[k],
                send_sem.at[w, 3 + k],
                recv_sem.at[w, 3 + k],
                z_peers[k][1],
            )
            for k in range(NZ - 1)
        ]
        half = total[w].shape[0]
        rows = pl.ds(pl.multiple_of(core * half, half), half)
        across = push(total[w], outs[w].at[rows], send_sem.at[w, 6], recv_sem.at[w, 6], to_other)
        store = pltpu.make_async_copy(total[w], outs[w].at[rows], load_sem.at[w, 2])
        load_a = pltpu.make_async_copy(parts[w].at[:, y, x], held[w].at[0], load_sem.at[w, 0])
        load_b = pltpu.make_async_copy(parts[w].at[:, y1, x1], held[w].at[1], load_sem.at[w, 1])
        plan.append((far_a, far_b, near, along_z, across, store, load_a, load_b))
        far_b.start()
        load_b.start()
        far_a.start()
        load_a.start()

    column = heads.at[:, y, x]
    column_first = heads.at[:, y1, x1]
    head_near = push(column, column, head_send.at[3], head_recv.at[3], to_first)
    head_far_a = push(column, column, head_send.at[4], head_recv.at[4], to_second)
    head_far_b = push(column_first, column_first, head_send.at[5], head_recv.at[5], to_second)
    for copy in head_z:
        copy.wait_recv()
    head_near.start()
    head_far_a.start()
    head_near.wait_recv()
    head_far_b.start()

    f32 = jnp.float32
    for step in range(count + 2):
        if step < count:
            w = step
            _, far_b, near, _, _, _, _, load_b = plan[w]
            load_b.wait()
            far_b.wait_recv()

            @pl.loop(0, NZ)
            def _(k, w=w):
                mine = held[w][1, k].astype(f32)
                held[w][1, k] = (mine + got_second[w][1, k].astype(f32)).astype(held[w].dtype)

            near.start()
        if 1 <= step <= count:
            w = step - 1
            far_a, _, near, along_z, _, _, load_a, _ = plan[w]
            load_a.wait()
            far_a.wait_recv()
            near.wait_recv()

            @pl.loop(0, NZ)
            def _(k, w=w):
                mine = held[w][0, k].astype(f32) + got_second[w][0, k].astype(f32)
                held[w][0, k] = (mine + got_first[w][k].astype(f32)).astype(held[w].dtype)

            for copy in along_z:
                copy.start()
        if step >= 2:
            w = step - 2
            _, _, _, along_z, across, store, _, _ = plan[w]
            for copy in along_z:
                copy.wait_recv()
            result = held[w][0, z].astype(f32)
            for k in range(NZ - 1):
                result = result + got_z[w][k].astype(f32)
            total[w][...] = result
            across.start()
            store.start()

    head_far_a.wait_recv()
    head_far_b.wait_recv()
    head_sum = heads[0, 0, 0]
    for k in range(1, GRID):
        head_sum = head_sum + heads[k // (NY * NX), (k // NX) % NY, k % NX]
    head_out[...] = head_sum
    for copy in head_z + [head_near, head_far_a, head_far_b]:
        copy.wait_send()
    for far_a, far_b, near, along_z, across, store, _, _ in plan:
        far_a.wait_send()
        far_b.wait_send()
        near.wait_send()
        for copy in along_z:
            copy.wait_send()
        across.wait()
        store.wait()


def scatter_all(head_part, parts):
    count = len(parts)
    units = [(part.shape[3:], part.dtype) for part in parts]
    scratch = [pltpu.VMEM((2, NZ) + shape, dtype) for shape, dtype in units]
    scratch += [pltpu.VMEM((2, NZ) + shape, dtype) for shape, dtype in units]
    scratch += [pltpu.VMEM((NZ,) + shape, dtype) for shape, dtype in units]
    scratch += [pltpu.VMEM((NZ - 1,) + shape, dtype) for shape, dtype in units]
    scratch += [pltpu.VMEM(shape, jnp.float32) for shape, dtype in units]
    scratch += [
        pltpu.VMEM((NZ, NY, NX) + head_part.shape, jnp.float32),
        pltpu.SemaphoreType.DMA((count, 3)),
        pltpu.SemaphoreType.DMA((count, 7)),
        pltpu.SemaphoreType.DMA((count, 7)),
        pltpu.SemaphoreType.DMA((6,)),
        pltpu.SemaphoreType.DMA((6,)),
    ]
    result = pl.pallas_call(
        functools.partial(scatter_kernel, count),
        out_shape=[jax.ShapeDtypeStruct(head_part.shape, jnp.float32)]
        + [
            jax.ShapeDtypeStruct((2 * shape[0],) + tuple(shape[1:]), jnp.float32)
            for shape, dtype in units
        ],
        in_specs=[pl.BlockSpec(memory_space=pltpu.VMEM)]
        + [pl.BlockSpec(memory_space=pl.ANY)] * count,
        out_specs=[pl.BlockSpec(memory_space=pltpu.VMEM)]
        + [pl.BlockSpec(memory_space=pl.ANY)] * count,
        scratch_shapes=scratch,
        compiler_params=pltpu.CompilerParams(
            collective_id=1, has_side_effects=True, vmem_limit_bytes=44 * 1024 * 1024
        ),
        name="scatter_gradients",
    )(head_part, *parts)
    return result[0], result[1:]


SMALL_ROWS = 32


def pack_small(pieces):
    rows = jnp.concatenate(pieces, axis=1)
    spare = SMALL_ROWS * 128 - rows.shape[1]
    return jnp.pad(rows, ((0, 0), (0, spare)))


def on_device_grid(
    hidden_in,
    seq_lengths,
    out_grad,
    in_gain,
    mixer_in,
    conv_weight,
    conv_bias,
    head_params,
    mixer_gain,
    mixer_out,
    qkv_weight,
    attn_out,
    ffn_gain,
    gate_up,
    ffn_down,
):
    small = pack_small(
        [
            in_gain[None],
            conv_weight.reshape(1, -1),
            conv_bias[None],
            mixer_gain[None],
            ffn_gain[None],
        ]
    ).reshape(SMALL_ROWS, 128)
    small_all, qkv_all, mixer_in_all, mixer_out_all, gate_up_all, ffn_down_all, attn_out_all = (
        gather_all([small, qkv_weight, mixer_in, mixer_out, gate_up, ffn_down, attn_out])
    )
    small_all = small_all.reshape(GRID, SMALL_ROWS * 128)
    d_loc, c_loc, m_loc = in_gain.shape[0], conv_bias.shape[0], mixer_gain.shape[0]
    marks = [0]
    for width in (d_loc, CONV * c_loc, c_loc, m_loc, d_loc):
        marks.append(marks[-1] + width)
    cuts = [small_all[:, marks[k] : marks[k + 1]] for k in range(5)]
    conv_all = cuts[1].reshape(GRID, CONV, c_loc).transpose(1, 0, 2).reshape(CONV, XBC)
    gathered = (
        cuts[0].reshape(-1),
        mixer_in_all,
        conv_all,
        cuts[2].reshape(-1),
        cuts[3].reshape(-1),
        mixer_out_all,
        qkv_all,
        attn_out_all,
        cuts[4].reshape(-1),
        gate_up_all,
        ffn_down_all,
    )
    hidden_out, input_grad, pairs, smalls = jax.vmap(
        lambda tokens, lengths, cotangent: micro_step(
            tokens, lengths, cotangent, gathered, head_params
        )
    )(hidden_in, seq_lengths[:, 0], out_grad)
    smalls = jax.tree.map(lambda value: jnp.sum(value, axis=0), smalls)
    core = lax.axis_index("rep")
    swap = [(0, 1), (1, 0)]

    def flat(rows):
        return rows.reshape(-1, rows.shape[-1])

    def both_right(rows):
        rows = flat(rows)
        return jnp.concatenate([rows, lax.ppermute(rows, "rep", swap)], axis=0)

    def both_left(rows):
        rows = flat(rows)
        tokens, width = rows.shape
        cut = rows.reshape(tokens, GRID, 2, width // (2 * GRID))
        front = cut[:, :, 0].reshape(tokens, width // 2)
        back = cut[:, :, 1].reshape(tokens, width // 2)
        keep = jnp.where(core == 0, front, back)
        give = jnp.where(core == 0, back, front)
        return jnp.concatenate([keep, lax.ppermute(give, "rep", swap)], axis=0)

    def half_grad(left, right):
        part = dot_left(left, right).astype(jnp.bfloat16)
        return part.reshape(NZ, NY, NX, part.shape[0] // GRID, part.shape[1])

    normed, grad_proj = both_left(pairs[0][0]), both_right(pairs[0][1])
    mixed_low, grad_res_low = both_left(pairs[1][0]), both_right(pairs[1][1])
    grad_qkv = both_right(pairs[2][1])
    attended = both_left(pairs[3][0])
    normed_two, grad_gu = both_left(pairs[4][0]), both_right(pairs[4][1])
    activated, cotangent = both_left(pairs[5][0]), both_right(pairs[5][1])
    grad_gain_one, grad_conv_weight, grad_conv_bias, grad_gain_mix, grad_gain_two, grad_head = (
        smalls
    )
    packet = pack_small(
        [
            grad_gain_one.reshape(GRID, d_loc),
            grad_conv_weight.reshape(CONV, GRID, c_loc).transpose(1, 0, 2).reshape(GRID, -1),
            grad_conv_bias.reshape(GRID, c_loc),
            grad_gain_mix.reshape(GRID, m_loc),
            grad_gain_two.reshape(GRID, d_loc),
        ]
    )
    head_row = jnp.pad(grad_head.reshape(1, -1), ((0, 0), (0, 1024 - 3 * HEADS)))
    own_small = jnp.concatenate(
        [packet[:, :1024].reshape(GRID * 8, 128), head_row.reshape(8, 128)], axis=0
    )
    chip_small = own_small + lax.ppermute(own_small, "rep", swap)
    small_part = chip_small[: GRID * 8].reshape(GRID, 8, 128)
    small_part = jnp.where(core == 0, small_part, 0.0).reshape(NZ, NY, NX, 8, 128)
    head_sum, sums = scatter_all(
        chip_small[GRID * 8 :],
        [
            small_part,
            half_grad(normed, grad_qkv),
            half_grad(normed, grad_proj),
            half_grad(mixed_low, grad_res_low),
            half_grad(normed_two, grad_gu),
            half_grad(activated, cotangent),
            half_grad(attended, grad_res_low),
        ],
    )
    row = sums[0].reshape(2, 1024)[0]
    cuts = [row[marks[k] : marks[k + 1]] for k in range(5)]
    return (
        hidden_out,
        input_grad,
        cuts[0],
        sums[2],
        cuts[1].reshape(CONV, c_loc),
        cuts[2],
        head_sum.reshape(-1)[: 3 * HEADS].reshape(3, HEADS),
        cuts[3],
        sums[3],
        sums[1],
        sums[6],
        cuts[4],
        sums[4],
        sums[5],
    )


def solution(mesh):
    grid = mesh.shape["fsdp"] == GRID and mesh.shape["rep"] == 2
    return jax.shard_map(
        on_device_grid if grid else on_device_any,
        mesh=mesh,
        in_specs=(
            P(None, ("fsdp", "rep"), None),
            P(None, ("fsdp", "rep"), None),
            P(None, ("fsdp", "rep"), None),
            P("fsdp"),
            P("fsdp", None),
            P(None, "fsdp"),
            P("fsdp"),
            P(),
            P("fsdp"),
            P("fsdp", None),
            P("fsdp", None),
            P("fsdp", None),
            P("fsdp"),
            P("fsdp", None),
            P("fsdp", None),
        ),
        out_specs=(
            P(None, ("fsdp", "rep"), None),
            P(None, ("fsdp", "rep"), None),
            P("fsdp"),
            P("fsdp", None),
            P(None, "fsdp"),
            P("fsdp"),
            P(),
            P("fsdp"),
            P("fsdp", None),
            P("fsdp", None),
            P("fsdp", None),
            P("fsdp"),
            P("fsdp", None),
            P("fsdp", None),
        ),
        check_vma=False,
    )
```

```python
import functools
import math

import jax
import jax.numpy as jnp
from jax import lax
from jax.experimental import pallas as pl
from jax.experimental.pallas import tpu as pltpu
from jax.sharding import PartitionSpec as P

HEADS = 24
HEAD_DIM = 64
STATE = 128
CONV = 4
QUERY_HEADS = 8
KEY_VALUE_HEADS = 2
HEAD_SIZE = 64
FF = 2048
MICRO = 2
DSSM = 1536
XBC = 1792


epsilon = 1e-05
highest = lax.Precision.HIGHEST
rope_base = 10000.0


def dot_bf(left, right):
    return jnp.dot(left, right, preferred_element_type=jnp.float32)


def dot_left(left, right):
    return lax.dot_general(
        left, right, (((0,), (0,)), ((), ())), preferred_element_type=jnp.float32
    )


def dot_right(left, right):
    return lax.dot_general(
        left, right, (((1,), (1,)), ((), ())), preferred_element_type=jnp.float32
    )


def rms_scale(value_rows):
    return lax.rsqrt(jnp.mean(value_rows * value_rows, axis=1, keepdims=True) + epsilon)


def norm_back(grad_normed, value_rows, scale_rows, gain_row):
    weighted = grad_normed * gain_row[None, :]
    inner_mean = jnp.mean(weighted * value_rows, axis=1, keepdims=True)
    return scale_rows * weighted - value_rows * scale_rows * scale_rows * scale_rows * inner_mean


def silu_slope(value_rows):
    sigma_v = jax.nn.sigmoid(value_rows)
    return sigma_v * (1.0 + value_rows * (1.0 - sigma_v))


def layout(lengths, count_of_tokens):
    seq_ends = jnp.cumsum(lengths, dtype=jnp.int32)
    places = jnp.arange(count_of_tokens, dtype=jnp.int32)
    passed = (places[:, None] >= seq_ends[None, :]).astype(jnp.int32)
    segment = jnp.sum(passed, axis=1, dtype=jnp.int32)
    starts = jnp.sum(passed * lengths[None, :], axis=1, dtype=jnp.int32)
    return (segment, places - starts)


def delay_keep(segment, lag_rows):
    count_of_tokens = segment.shape[0]
    earlier = jnp.concatenate(
        [jnp.full((lag_rows,), -1, jnp.int32), segment[: count_of_tokens - lag_rows]], axis=0
    )
    return earlier == segment


def delayed(value_rows, segment, lag_rows):
    count_of_tokens = value_rows.shape[0]
    shifted = jnp.concatenate(
        [
            jnp.zeros((lag_rows, value_rows.shape[1]), value_rows.dtype),
            value_rows[: count_of_tokens - lag_rows],
        ],
        axis=0,
    )
    return jnp.where(delay_keep(segment, lag_rows)[:, None], shifted, 0.0)


def rotary(position):
    half_width = HEAD_SIZE // 2
    inverse_freq = jnp.exp(
        jnp.arange(half_width, dtype=jnp.float32) * (-2.0 * math.log(rope_base) / HEAD_SIZE)
    )
    angles = position.astype(jnp.float32)[:, None] * inverse_freq[None, :]
    cosine_table = jnp.concatenate([jnp.cos(angles), jnp.cos(angles)], axis=1)
    sine_table = jnp.concatenate([jnp.sin(angles), jnp.sin(angles)], axis=1)
    return (cosine_table, sine_table)


def rotate(value_rows):
    first_half, second_half = jnp.split(value_rows, 2, axis=-1)
    return jnp.concatenate([-second_half, first_half], axis=-1)


def rotate_back(value_rows):
    first_half, second_half = jnp.split(value_rows, 2, axis=-1)
    return jnp.concatenate([second_half, -first_half], axis=-1)


def collect(
    in_gain,
    mixer_in,
    conv_weight,
    conv_bias,
    mixer_gain,
    mixer_out,
    qkv_weight,
    attn_out,
    ffn_gain,
    gate_up,
    ffn_down,
):
    return (
        lax.all_gather(in_gain, "fsdp", axis=0, tiled=True),
        lax.all_gather(mixer_in, "fsdp", axis=0, tiled=True),
        lax.all_gather(conv_weight, "fsdp", axis=1, tiled=True),
        lax.all_gather(conv_bias, "fsdp", axis=0, tiled=True),
        lax.all_gather(mixer_gain, "fsdp", axis=0, tiled=True),
        lax.all_gather(mixer_out, "fsdp", axis=0, tiled=True),
        lax.all_gather(qkv_weight, "fsdp", axis=0, tiled=True),
        lax.all_gather(attn_out, "fsdp", axis=0, tiled=True),
        lax.all_gather(ffn_gain, "fsdp", axis=0, tiled=True),
        lax.all_gather(gate_up, "fsdp", axis=0, tiled=True),
        lax.all_gather(ffn_down, "fsdp", axis=0, tiled=True),
    )


def micro_step(tokens, lengths, cotangent, gathered, head_params):
    (
        in_gain,
        mixer_in,
        conv_weight,
        conv_bias,
        mixer_gain,
        mixer_out,
        qkv_weight,
        attn_out,
        ffn_gain,
        gate_up,
        ffn_down,
    ) = gathered
    count_of_tokens = tokens.shape[0]
    x_float = tokens.astype(jnp.float32)
    segment, position = layout(lengths, count_of_tokens)
    places = jnp.arange(count_of_tokens, dtype=jnp.int32)
    visible = (segment[:, None] == segment[None, :]) & (places[:, None] >= places[None, :])
    gain_one = in_gain.astype(jnp.float32)
    scale_one = rms_scale(x_float)
    normed = (x_float * scale_one * gain_one[None, :]).astype(jnp.bfloat16)
    projected = dot_bf(normed, mixer_in)
    gate_z = projected[:, :DSSM]
    conv_input = projected[:, DSSM : DSSM + XBC]
    step_raw = projected[:, DSSM + XBC :]
    conv_taps = conv_weight.astype(jnp.float32)
    conv_sum = jnp.broadcast_to(conv_bias.astype(jnp.float32)[None, :], (count_of_tokens, XBC))
    tap_inputs = []
    for offset in range(CONV):
        tap_value = delayed(conv_input, segment, CONV - 1 - offset)
        tap_inputs.append(tap_value)
        conv_sum = conv_sum + conv_taps[offset][None, :] * tap_value
    conv_out = jax.nn.silu(conv_sum)
    inner_x = conv_out[:, :DSSM].reshape(count_of_tokens, HEADS, HEAD_DIM)
    input_b = conv_out[:, DSSM : DSSM + STATE]
    input_c = conv_out[:, DSSM + STATE :]
    step_in = step_raw + head_params[0][None, :]
    step_size = jax.nn.softplus(step_in)
    decay_rate = -jnp.exp(head_params[1])
    skip_factor = head_params[2]
    cumulative = jnp.cumsum(step_size * decay_rate[None, :], axis=0)
    inside = visible[:, :, None]
    decay_mask = jnp.where(
        inside,
        jnp.exp(jnp.where(inside, cumulative[:, None, :] - cumulative[None, :, :], 0.0)),
        0.0,
    )
    intersection = jnp.dot(input_c, input_b.T, precision=highest)
    mixing = intersection[:, :, None] * decay_mask
    scaled_in = inner_x * step_size[:, :, None]
    ssd_out = (
        jnp.einsum("tsh,shp->thp", mixing, scaled_in, precision=highest)
        + skip_factor[None, :, None] * inner_x
    )
    flat_ssd = ssd_out.reshape(count_of_tokens, DSSM)
    silu_z = jax.nn.silu(gate_z)
    gated_out = flat_ssd * silu_z
    gain_mix = mixer_gain.astype(jnp.float32)
    scale_two = rms_scale(gated_out)
    mixed_low = (gated_out * scale_two * gain_mix[None, :]).astype(jnp.bfloat16)
    mixer_branch = dot_bf(mixed_low, mixer_out)
    query_key_value_output = dot_bf(normed, qkv_weight)
    query_group_width = QUERY_HEADS // KEY_VALUE_HEADS
    query_rows = query_key_value_output[:, : QUERY_HEADS * HEAD_SIZE].reshape(
        count_of_tokens, KEY_VALUE_HEADS, query_group_width, HEAD_SIZE
    )
    key_matrix_rows = query_key_value_output[
        :, QUERY_HEADS * HEAD_SIZE : (QUERY_HEADS + KEY_VALUE_HEADS) * HEAD_SIZE
    ].reshape(count_of_tokens, KEY_VALUE_HEADS, HEAD_SIZE)
    value_rows = query_key_value_output[:, (QUERY_HEADS + KEY_VALUE_HEADS) * HEAD_SIZE :].reshape(
        count_of_tokens, KEY_VALUE_HEADS, HEAD_SIZE
    )
    cosine_table, sine_table = rotary(position)
    rot_q = (
        query_rows * cosine_table[:, None, None, :]
        + rotate(query_rows) * sine_table[:, None, None, :]
    ).astype(jnp.bfloat16)
    rot_k = (
        key_matrix_rows * cosine_table[:, None, :]
        + rotate(key_matrix_rows) * sine_table[:, None, :]
    ).astype(jnp.bfloat16)
    value_low = value_rows.astype(jnp.bfloat16)
    score_scale = HEAD_SIZE ** (-0.5)
    scores = (
        jnp.einsum("tkgd,skd->kgts", rot_q, rot_k, preferred_element_type=jnp.float32) * score_scale
    )
    scores = jnp.where(visible[None, None], scores, -1e30)
    exponent = jnp.exp(scores - jnp.max(scores, axis=3, keepdims=True))
    attention_probs = exponent / jnp.sum(exponent, axis=3, keepdims=True)
    probs_low = attention_probs.astype(jnp.bfloat16)
    attended = jnp.einsum(
        "kgts,skd->tkgd", probs_low, value_low, preferred_element_type=jnp.float32
    )
    attended = attended.reshape(count_of_tokens, QUERY_HEADS * HEAD_SIZE).astype(jnp.bfloat16)
    attn_branch = dot_bf(attended, attn_out)
    residual = x_float + mixer_branch + attn_branch
    gain_two = ffn_gain.astype(jnp.float32)
    scale_three = rms_scale(residual)
    normed_two = (residual * scale_three * gain_two[None, :]).astype(jnp.bfloat16)
    gate_upv = dot_bf(normed_two, gate_up)
    gate_part = gate_upv[:, :FF]
    up_part = gate_upv[:, FF:]
    activated = (jax.nn.silu(gate_part) * up_part).astype(jnp.bfloat16)
    ffn_branch = dot_bf(activated, ffn_down)
    output = (residual + ffn_branch).astype(jnp.bfloat16)
    grad_out = cotangent.astype(jnp.float32)
    grad_act = dot_right(cotangent, ffn_down)
    grad_gu = jnp.concatenate(
        [grad_act * up_part * silu_slope(gate_part), grad_act * jax.nn.silu(gate_part)], axis=1
    ).astype(jnp.bfloat16)
    grad_n_two = dot_right(grad_gu, gate_up)
    grad_gain_two = jnp.sum(grad_n_two * residual * scale_three, axis=0)
    grad_residual = grad_out + norm_back(grad_n_two, residual, scale_three, gain_two)
    grad_res_low = grad_residual.astype(jnp.bfloat16)
    grad_att = (
        dot_right(grad_res_low, attn_out)
        .astype(jnp.bfloat16)
        .reshape(count_of_tokens, KEY_VALUE_HEADS, query_group_width, HEAD_SIZE)
    )
    value_gradient = jnp.einsum(
        "kgts,tkgd->skd", probs_low, grad_att, preferred_element_type=jnp.float32
    )
    grad_probs = jnp.einsum(
        "tkgd,skd->kgts", grad_att, value_low, preferred_element_type=jnp.float32
    )
    grad_scores = attention_probs * (
        grad_probs - jnp.sum(grad_probs * attention_probs, axis=3, keepdims=True)
    )
    grad_scores_low = grad_scores.astype(jnp.bfloat16)
    grad_rot_q = (
        jnp.einsum("kgts,skd->tkgd", grad_scores_low, rot_k, preferred_element_type=jnp.float32)
        * score_scale
    )
    grad_rot_k = (
        jnp.einsum("kgts,tkgd->skd", grad_scores_low, rot_q, preferred_element_type=jnp.float32)
        * score_scale
    )
    grad_q = grad_rot_q * cosine_table[:, None, None, :] + rotate_back(
        grad_rot_q * sine_table[:, None, None, :]
    )
    key_gradient = grad_rot_k * cosine_table[:, None, :] + rotate_back(
        grad_rot_k * sine_table[:, None, :]
    )
    grad_qkv = jnp.concatenate(
        [
            grad_q.reshape(count_of_tokens, QUERY_HEADS * HEAD_SIZE),
            key_gradient.reshape(count_of_tokens, KEY_VALUE_HEADS * HEAD_SIZE),
            value_gradient.reshape(count_of_tokens, KEY_VALUE_HEADS * HEAD_SIZE),
        ],
        axis=1,
    ).astype(jnp.bfloat16)
    grad_mixed = dot_right(grad_res_low, mixer_out)
    grad_gain_mix = jnp.sum(grad_mixed * gated_out * scale_two, axis=0)
    grad_gated = norm_back(grad_mixed, gated_out, scale_two, gain_mix)
    grad_ssd = (grad_gated * silu_z).reshape(count_of_tokens, HEADS, HEAD_DIM)
    grad_z = grad_gated * flat_ssd * silu_slope(gate_z)
    grad_skip = jnp.sum(grad_ssd * inner_x, axis=(0, 2))
    grad_scaled = jnp.einsum("tsh,thp->shp", mixing, grad_ssd, precision=highest)
    grad_mixing = jnp.einsum("thp,shp->tsh", grad_ssd, scaled_in, precision=highest)
    grad_intersection = jnp.sum(grad_mixing * decay_mask, axis=2)
    grad_differ = grad_mixing * mixing
    grad_cumul = jnp.sum(grad_differ, axis=1) - jnp.sum(grad_differ, axis=0)
    grad_logs = jnp.cumsum(grad_cumul[::-1], axis=0)[::-1]
    grad_delta = grad_logs * decay_rate[None, :] + jnp.sum(grad_scaled * inner_x, axis=2)
    grad_rate_log = jnp.sum(grad_logs * step_size, axis=0) * decay_rate
    grad_inner = grad_scaled * step_size[:, :, None] + skip_factor[None, :, None] * grad_ssd
    grad_step = grad_delta * jax.nn.sigmoid(step_in)
    grad_head = jnp.stack([jnp.sum(grad_step, axis=0), grad_rate_log, grad_skip], axis=0)
    grad_c = jnp.dot(grad_intersection, input_b, precision=highest)
    grad_b = jnp.dot(grad_intersection.T, input_c, precision=highest)
    grad_conv_out = jnp.concatenate(
        [grad_inner.reshape(count_of_tokens, DSSM), grad_b, grad_c], axis=1
    )
    grad_conv_sum = grad_conv_out * silu_slope(conv_sum)
    grad_conv_bias = jnp.sum(grad_conv_sum, axis=0)
    grad_conv_weight = jnp.stack(
        [jnp.sum(grad_conv_sum * tap_inputs[offset], axis=0) for offset in range(CONV)], axis=0
    )
    grad_conv_in = jnp.zeros((count_of_tokens, XBC), jnp.float32)
    for offset in range(CONV):
        lag_rows = CONV - 1 - offset
        tap_term = jnp.where(
            delay_keep(segment, lag_rows)[:, None], grad_conv_sum * conv_taps[offset][None, :], 0.0
        )
        grad_conv_in = grad_conv_in + jnp.concatenate(
            [tap_term[lag_rows:], jnp.zeros((lag_rows, XBC), jnp.float32)], axis=0
        )
    grad_proj = jnp.concatenate([grad_z, grad_conv_in, grad_step], axis=1).astype(jnp.bfloat16)
    grad_normed = dot_right(grad_proj, mixer_in) + dot_right(grad_qkv, qkv_weight)
    grad_gain_one = jnp.sum(grad_normed * x_float * scale_one, axis=0)
    grad_input = grad_residual + norm_back(grad_normed, x_float, scale_one, gain_one)
    pairs = (
        (normed, grad_proj),
        (mixed_low, grad_res_low),
        (normed, grad_qkv),
        (attended, grad_res_low),
        (normed_two, grad_gu),
        (activated, cotangent),
    )
    smalls = (
        grad_gain_one,
        grad_conv_weight,
        grad_conv_bias,
        grad_gain_mix,
        grad_gain_two,
        grad_head,
    )
    return (output, grad_input, pairs, smalls)


def on_device_any(
    hidden_in,
    seq_lengths,
    out_grad,
    in_gain,
    mixer_in,
    conv_weight,
    conv_bias,
    head_params,
    mixer_gain,
    mixer_out,
    qkv_weight,
    attn_out,
    ffn_gain,
    gate_up,
    ffn_down,
):
    gathered = None
    gathered = collect(
        in_gain,
        mixer_in,
        conv_weight,
        conv_bias,
        mixer_gain,
        mixer_out,
        qkv_weight,
        attn_out,
        ffn_gain,
        gate_up,
        ffn_down,
    )
    outputs = []
    input_grads = []
    kept_rows = []
    small_total = None
    for micro_index in range(MICRO):
        output, grad_input, pairs, smalls = micro_step(
            hidden_in[micro_index],
            seq_lengths[micro_index, 0],
            out_grad[micro_index],
            gathered,
            head_params,
        )
        outputs.append(output)
        input_grads.append(grad_input)
        kept_rows.append(pairs)
        small_total = smalls if small_total is None else jax.tree.map(jnp.add, small_total, smalls)
    full_grads = []
    for pair_index in range(6):
        left_rows = jnp.concatenate(
            [kept_rows[micro_index][pair_index][0] for micro_index in range(MICRO)], axis=0
        )
        right_rows = jnp.concatenate(
            [kept_rows[micro_index][pair_index][1] for micro_index in range(MICRO)], axis=0
        )
        full_grads.append(dot_left(left_rows, right_rows))
    grad_gain_one, grad_conv_weight, grad_conv_bias, grad_gain_mix, grad_gain_two, grad_head = (
        small_total
    )
    grad_terms = (
        grad_gain_one,
        full_grads[0],
        grad_conv_weight,
        grad_conv_bias,
        grad_gain_mix,
        full_grads[1],
        full_grads[2],
        full_grads[3],
        grad_gain_two,
        full_grads[4],
        full_grads[5],
    )
    shard_grads = (
        lax.psum_scatter(grad_terms[0], "fsdp", scatter_dimension=0, tiled=True),
        lax.psum_scatter(grad_terms[1], "fsdp", scatter_dimension=0, tiled=True),
        lax.psum_scatter(grad_terms[2], "fsdp", scatter_dimension=1, tiled=True),
        lax.psum_scatter(grad_terms[3], "fsdp", scatter_dimension=0, tiled=True),
        lax.psum_scatter(grad_terms[4], "fsdp", scatter_dimension=0, tiled=True),
        lax.psum_scatter(grad_terms[5], "fsdp", scatter_dimension=0, tiled=True),
        lax.psum_scatter(grad_terms[6], "fsdp", scatter_dimension=0, tiled=True),
        lax.psum_scatter(grad_terms[7], "fsdp", scatter_dimension=0, tiled=True),
        lax.psum_scatter(grad_terms[8], "fsdp", scatter_dimension=0, tiled=True),
        lax.psum_scatter(grad_terms[9], "fsdp", scatter_dimension=0, tiled=True),
        lax.psum_scatter(grad_terms[10], "fsdp", scatter_dimension=0, tiled=True),
    )
    halves = (
        lax.psum_scatter(
            shard_grads[0].astype(jnp.bfloat16), "rep", scatter_dimension=0, tiled=True
        ).astype(jnp.float32),
        lax.psum_scatter(
            shard_grads[1].astype(jnp.bfloat16), "rep", scatter_dimension=0, tiled=True
        ).astype(jnp.float32),
        lax.psum_scatter(
            shard_grads[2].astype(jnp.bfloat16), "rep", scatter_dimension=1, tiled=True
        ).astype(jnp.float32),
        lax.psum_scatter(
            shard_grads[3].astype(jnp.bfloat16), "rep", scatter_dimension=0, tiled=True
        ).astype(jnp.float32),
        lax.psum_scatter(
            shard_grads[4].astype(jnp.bfloat16), "rep", scatter_dimension=0, tiled=True
        ).astype(jnp.float32),
        lax.psum_scatter(
            shard_grads[5].astype(jnp.bfloat16), "rep", scatter_dimension=0, tiled=True
        ).astype(jnp.float32),
        lax.psum_scatter(
            shard_grads[6].astype(jnp.bfloat16), "rep", scatter_dimension=0, tiled=True
        ).astype(jnp.float32),
        lax.psum_scatter(
            shard_grads[7].astype(jnp.bfloat16), "rep", scatter_dimension=0, tiled=True
        ).astype(jnp.float32),
        lax.psum_scatter(
            shard_grads[8].astype(jnp.bfloat16), "rep", scatter_dimension=0, tiled=True
        ).astype(jnp.float32),
        lax.psum_scatter(
            shard_grads[9].astype(jnp.bfloat16), "rep", scatter_dimension=0, tiled=True
        ).astype(jnp.float32),
        lax.psum_scatter(
            shard_grads[10].astype(jnp.bfloat16), "rep", scatter_dimension=0, tiled=True
        ).astype(jnp.float32),
    )
    head_total = lax.psum(grad_head, ("fsdp", "rep"))
    summed = (
        lax.all_gather(halves[0].astype(jnp.bfloat16), "rep", axis=0, tiled=True).astype(
            jnp.float32
        ),
        lax.all_gather(halves[1].astype(jnp.bfloat16), "rep", axis=0, tiled=True).astype(
            jnp.float32
        ),
        lax.all_gather(halves[2].astype(jnp.bfloat16), "rep", axis=1, tiled=True).astype(
            jnp.float32
        ),
        lax.all_gather(halves[3].astype(jnp.bfloat16), "rep", axis=0, tiled=True).astype(
            jnp.float32
        ),
        lax.all_gather(halves[4].astype(jnp.bfloat16), "rep", axis=0, tiled=True).astype(
            jnp.float32
        ),
        lax.all_gather(halves[5].astype(jnp.bfloat16), "rep", axis=0, tiled=True).astype(
            jnp.float32
        ),
        lax.all_gather(halves[6].astype(jnp.bfloat16), "rep", axis=0, tiled=True).astype(
            jnp.float32
        ),
        lax.all_gather(halves[7].astype(jnp.bfloat16), "rep", axis=0, tiled=True).astype(
            jnp.float32
        ),
        lax.all_gather(halves[8].astype(jnp.bfloat16), "rep", axis=0, tiled=True).astype(
            jnp.float32
        ),
        lax.all_gather(halves[9].astype(jnp.bfloat16), "rep", axis=0, tiled=True).astype(
            jnp.float32
        ),
        lax.all_gather(halves[10].astype(jnp.bfloat16), "rep", axis=0, tiled=True).astype(
            jnp.float32
        ),
    )
    hidden_out = jnp.stack(outputs, axis=0)
    input_grad = jnp.stack(input_grads, axis=0)
    return (
        hidden_out,
        input_grad,
        summed[0],
        summed[1],
        summed[2],
        summed[3],
        head_total,
        summed[4],
        summed[5],
        summed[6],
        summed[7],
        summed[8],
        summed[9],
        summed[10],
    )


MESH = pl.DeviceIdType.MESH
NZ, NY, NX = 4, 2, 2
GRID = NZ * NY * NX


def positions():
    chip = lax.axis_index("fsdp")
    core = lax.axis_index("rep")
    z = chip // (NY * NX)
    y = (chip // NX) % NY
    x = chip % NX
    y1 = (y + core) % 2
    x1 = (x + 1 - core) % 2
    y2 = (y + 1 - core) % 2
    x2 = (x + core) % 2
    return z, y, x, y1, x1, y2, x2, core


def chip_of(z, y, x):
    return (z * NY + y) * NX + x


def greet(z, y, x, y1, x1, y2, x2, core):
    barrier = pltpu.get_barrier_semaphore()
    partners = [(chip_of((z + dz) % NZ, y, x), core) for dz in range(1, NZ)]
    partners += [(chip_of(z, y1, x1), core), (chip_of(z, y2, x2), core)]
    partners += [(chip_of(z, y, x), 1 - core)]
    for partner in partners:
        pl.semaphore_signal(barrier, inc=1, device_id=partner, device_id_type=MESH)
    pl.semaphore_wait(barrier, len(partners))


def push(src_ref, dst_ref, send_sem, recv_sem, partner):
    return pltpu.make_async_remote_copy(
        src_ref=src_ref,
        dst_ref=dst_ref,
        send_sem=send_sem,
        recv_sem=recv_sem,
        device_id=partner,
        device_id_type=MESH,
    )


def gather_kernel(count, *refs):
    shards = refs[:count]
    wholes = refs[count : 2 * count]
    own_sem, send_sem, recv_sem = refs[2 * count :]
    z, y, x, y1, x1, y2, x2, core = positions()
    greet(z, y, x, y1, x1, y2, x2, core)
    to_first = (chip_of(z, y1, x1), core)
    to_second = (chip_of(z, y2, x2), core)
    to_other = (chip_of(z, y, x), 1 - core)
    plan = []
    for w in range(count):
        half = shards[w].shape[0] // 2
        rows = pl.ds(pl.multiple_of(core * half, half), half)
        whole = wholes[w]
        own = pltpu.make_async_copy(shards[w].at[rows], whole.at[z, y, x, rows], own_sem.at[w])
        along_z = [
            push(
                shards[w].at[rows],
                whole.at[z, y, x, rows],
                send_sem.at[w, dz - 1],
                recv_sem.at[w, dz - 1],
                (chip_of((z + dz) % NZ, y, x), core),
            )
            for dz in range(1, NZ)
        ]
        column = whole.at[:, y, x, rows]
        column_first = whole.at[:, y1, x1, rows]
        along_first = push(column, column, send_sem.at[w, 3], recv_sem.at[w, 3], to_first)
        second_a = push(column, column, send_sem.at[w, 4], recv_sem.at[w, 4], to_second)
        second_b = push(column_first, column_first, send_sem.at[w, 5], recv_sem.at[w, 5], to_second)
        half_all = whole.at[:, :, :, rows]
        across = push(half_all, half_all, send_sem.at[w, 6], recv_sem.at[w, 6], to_other)
        plan.append((own, along_z, along_first, second_a, second_b, across))
    for own, along_z, _, _, _, _ in plan:
        own.start()
        for copy in along_z:
            copy.start()
    for step in range(count + 2):
        if step < count:
            own, along_z, along_first, second_a, _, _ = plan[step]
            own.wait()
            for copy in along_z:
                copy.wait_recv()
            along_first.start()
            second_a.start()
        if 1 <= step <= count:
            _, _, along_first, _, second_b, _ = plan[step - 1]
            along_first.wait_recv()
            second_b.start()
        if step >= 2:
            _, _, _, second_a, second_b, across = plan[step - 2]
            second_a.wait_recv()
            second_b.wait_recv()
            across.start()
    for _, along_z, along_first, second_a, second_b, across in plan:
        for copy in along_z:
            copy.wait_send()
        along_first.wait_send()
        second_a.wait_send()
        second_b.wait_send()
        across.wait()


def gather_all(shards):
    count = len(shards)
    gathered = pl.pallas_call(
        functools.partial(gather_kernel, count),
        out_shape=[
            jax.ShapeDtypeStruct((NZ, NY, NX) + shard.shape, shard.dtype) for shard in shards
        ],
        in_specs=[pl.BlockSpec(memory_space=pl.ANY)] * count,
        out_specs=[pl.BlockSpec(memory_space=pl.ANY)] * count,
        scratch_shapes=[
            pltpu.SemaphoreType.DMA((count,)),
            pltpu.SemaphoreType.DMA((count, 7)),
            pltpu.SemaphoreType.DMA((count, 7)),
        ],
        compiler_params=pltpu.CompilerParams(collective_id=0, has_side_effects=True),
        name="gather_weights",
    )(*shards)
    return [
        whole.reshape((GRID * shard.shape[0],) + shard.shape[1:])
        for whole, shard in zip(gathered, shards)
    ]


CHUNK = 512


def scatter_kernel(pick, *refs):
    count = 1 + len(pick)
    lefts = 1 + max(left for left, _ in pick)
    rights = 1 + max(right for _, right in pick)
    head_ref, small_ref = refs[:2]
    left_refs = refs[2 : 2 + lefts]
    right_refs = refs[2 + lefts : 2 + lefts + rights]
    refs = refs[2 + lefts + rights :]
    head_out = refs[0]
    outs = refs[1 : 1 + count]
    rest = refs[1 + count :]
    grads = rest[:count]
    got_second = rest[count : 2 * count]
    got_first = rest[2 * count : 3 * count]
    got_z = rest[3 * count : 4 * count]
    total = rest[4 * count : 5 * count]
    heads, store_sem, send_sem, recv_sem, head_send, head_recv = rest[5 * count :]
    z, y, x, y1, x1, y2, x2, core = positions()
    targets = ((1 - y, 1 - x), (y2, x2), (y1, x1), (y, x))
    greet(z, y, x, y1, x1, y2, x2, core)
    to_first = (chip_of(z, y1, x1), core)
    to_second = (chip_of(z, y2, x2), core)
    to_other = (chip_of(z, y, x), 1 - core)
    z_peers = [((z + dz) % NZ, (chip_of((z + dz) % NZ, y, x), core)) for dz in range(1, NZ)]
    f32 = jnp.float32

    head_z = [
        push(head_ref, heads.at[z, y, x], head_send.at[k], head_recv.at[k], z_peers[k][1])
        for k in range(NZ - 1)
    ]
    for copy in head_z:
        copy.start()
    heads[z, y, x] = head_ref[...]

    def fill(w, place):
        row, column = targets[place]
        if w == 0:
            grads[0][place] = small_ref[:, row, column]
            return
        left_ref = left_refs[pick[w - 1][0]]
        right_ref = right_refs[pick[w - 1][1]]
        left = jnp.concatenate([left_ref[k, row, column] for k in range(NZ)], axis=0)
        width = right_ref.shape[1]
        half = left_ref.shape[3]

        def some(columns, size):
            block = jnp.dot(left, right_ref[:, columns], preferred_element_type=f32)
            block = block.astype(jnp.bfloat16)
            grads[w][place, :, :, columns] = block.reshape(NZ, half, size)

        @pl.loop(0, width // CHUNK)
        def _(step):
            some(pl.ds(pl.multiple_of(step * CHUNK, CHUNK), CHUNK), CHUNK)

        if width % CHUNK:
            some(pl.ds(width // CHUNK * CHUNK, width % CHUNK), width % CHUNK)

    plan = []
    for w in range(count):
        far = [
            push(
                grads[w].at[k],
                got_second[w].at[k],
                send_sem.at[w, k],
                recv_sem.at[w, k],
                to_second,
            )
            for k in range(2)
        ]
        near = push(grads[w].at[2], got_first[w], send_sem.at[w, 2], recv_sem.at[w, 2], to_first)
        along_z = [
            push(
                grads[w].at[3, z_peers[k][0]],
                got_z[w].at[k],
                send_sem.at[w, 3 + k],
                recv_sem.at[w, 3 + k],
                z_peers[k][1],
            )
            for k in range(NZ - 1)
        ]
        half = total[w].shape[0]
        rows = pl.ds(pl.multiple_of(core * half, half), half)
        across = push(total[w], outs[w].at[rows], send_sem.at[w, 6], recv_sem.at[w, 6], to_other)
        store = pltpu.make_async_copy(total[w], outs[w].at[rows], store_sem.at[w])
        plan.append((far, near, along_z, across, store))
        for k in range(2):
            fill(w, k)
            far[k].start()

    column = heads.at[:, y, x]
    column_first = heads.at[:, y1, x1]
    head_near = push(column, column, head_send.at[3], head_recv.at[3], to_first)
    head_far_a = push(column, column, head_send.at[4], head_recv.at[4], to_second)
    head_far_b = push(column_first, column_first, head_send.at[5], head_recv.at[5], to_second)
    for copy in head_z:
        copy.wait_recv()
    head_near.start()
    head_far_a.start()

    for w in range(count):
        fill(w, 2)
        fill(w, 3)

    head_near.wait_recv()
    head_far_b.start()

    for step in range(count + 2):
        if step < count:
            w = step
            far, near, _, _, _ = plan[w]
            far[0].wait_recv()

            @pl.loop(0, NZ)
            def _(k, w=w):
                mine = grads[w][2, k].astype(f32)
                grads[w][2, k] = (mine + got_second[w][0, k].astype(f32)).astype(grads[w].dtype)

            near.start()
        if 1 <= step <= count:
            w = step - 1
            far, near, along_z, _, _ = plan[w]
            far[1].wait_recv()
            near.wait_recv()

            @pl.loop(0, NZ)
            def _(k, w=w):
                mine = grads[w][3, k].astype(f32) + got_second[w][1, k].astype(f32)
                grads[w][3, k] = (mine + got_first[w][k].astype(f32)).astype(grads[w].dtype)

            for copy in along_z:
                copy.start()
        if step >= 2:
            w = step - 2
            _, _, along_z, across, store = plan[w]
            for copy in along_z:
                copy.wait_recv()
            result = grads[w][3, z].astype(f32)
            for k in range(NZ - 1):
                result = result + got_z[w][k].astype(f32)
            total[w][...] = result
            across.start()
            store.start()

    head_far_a.wait_recv()
    head_far_b.wait_recv()
    head_sum = heads[0, 0, 0]
    for k in range(1, GRID):
        head_sum = head_sum + heads[k // (NY * NX), (k // NX) % NY, k % NX]
    head_out[...] = head_sum
    for copy in head_z + [head_near, head_far_a, head_far_b]:
        copy.wait_send()
    for far, near, along_z, across, store in plan:
        for copy in far + [near] + along_z:
            copy.wait_send()
        across.wait()
        store.wait()


def scatter_all(head_part, small_part, lefts, rights, pick):
    count = 1 + len(pick)
    units = [(small_part.shape[3:], small_part.dtype)]
    for left, right in pick:
        units.append(((lefts[left].shape[3], rights[right].shape[1]), jnp.bfloat16))
    scratch = [pltpu.VMEM((4, NZ) + shape, dtype) for shape, dtype in units]
    scratch += [pltpu.VMEM((2, NZ) + shape, dtype) for shape, dtype in units]
    scratch += [pltpu.VMEM((NZ,) + shape, dtype) for shape, dtype in units]
    scratch += [pltpu.VMEM((NZ - 1,) + shape, dtype) for shape, dtype in units]
    scratch += [pltpu.VMEM(shape, jnp.float32) for shape, dtype in units]
    scratch += [
        pltpu.VMEM((NZ, NY, NX) + head_part.shape, jnp.float32),
        pltpu.SemaphoreType.DMA((count,)),
        pltpu.SemaphoreType.DMA((count, 7)),
        pltpu.SemaphoreType.DMA((count, 7)),
        pltpu.SemaphoreType.DMA((6,)),
        pltpu.SemaphoreType.DMA((6,)),
    ]
    operands = [head_part, small_part] + lefts + rights
    result = pl.pallas_call(
        functools.partial(scatter_kernel, pick),
        out_shape=[jax.ShapeDtypeStruct(head_part.shape, jnp.float32)]
        + [
            jax.ShapeDtypeStruct((2 * shape[0],) + tuple(shape[1:]), jnp.float32)
            for shape, dtype in units
        ],
        in_specs=[pl.BlockSpec(memory_space=pltpu.VMEM)] * len(operands),
        out_specs=[pl.BlockSpec(memory_space=pltpu.VMEM)]
        + [pl.BlockSpec(memory_space=pl.ANY)] * count,
        scratch_shapes=scratch,
        compiler_params=pltpu.CompilerParams(
            collective_id=1, has_side_effects=True, vmem_limit_bytes=50 * 1024 * 1024
        ),
        name="scatter_gradients",
    )(*operands)
    return result[0], result[1:]


SMALL_ROWS = 32


def pack_small(pieces):
    rows = jnp.concatenate(pieces, axis=1)
    spare = SMALL_ROWS * 128 - rows.shape[1]
    return jnp.pad(rows, ((0, 0), (0, spare)))


def on_device_grid(
    hidden_in,
    seq_lengths,
    out_grad,
    in_gain,
    mixer_in,
    conv_weight,
    conv_bias,
    head_params,
    mixer_gain,
    mixer_out,
    qkv_weight,
    attn_out,
    ffn_gain,
    gate_up,
    ffn_down,
):
    small = pack_small(
        [
            in_gain[None],
            conv_weight.reshape(1, -1),
            conv_bias[None],
            mixer_gain[None],
            ffn_gain[None],
        ]
    ).reshape(SMALL_ROWS, 128)
    small_all, qkv_all, mixer_in_all, mixer_out_all, gate_up_all, ffn_down_all, attn_out_all = (
        gather_all([small, qkv_weight, mixer_in, mixer_out, gate_up, ffn_down, attn_out])
    )
    small_all = small_all.reshape(GRID, SMALL_ROWS * 128)
    d_loc, c_loc, m_loc = in_gain.shape[0], conv_bias.shape[0], mixer_gain.shape[0]
    marks = [0]
    for width in (d_loc, CONV * c_loc, c_loc, m_loc, d_loc):
        marks.append(marks[-1] + width)
    cuts = [small_all[:, marks[k] : marks[k + 1]] for k in range(5)]
    conv_all = cuts[1].reshape(GRID, CONV, c_loc).transpose(1, 0, 2).reshape(CONV, XBC)
    gathered = (
        cuts[0].reshape(-1),
        mixer_in_all,
        conv_all,
        cuts[2].reshape(-1),
        cuts[3].reshape(-1),
        mixer_out_all,
        qkv_all,
        attn_out_all,
        cuts[4].reshape(-1),
        gate_up_all,
        ffn_down_all,
    )
    hidden_out, input_grad, pairs, smalls = jax.vmap(
        lambda tokens, lengths, cotangent: micro_step(
            tokens, lengths, cotangent, gathered, head_params
        )
    )(hidden_in, seq_lengths[:, 0], out_grad)
    smalls = jax.tree.map(lambda value: jnp.sum(value, axis=0), smalls)
    core = lax.axis_index("rep")
    swap = [(0, 1), (1, 0)]

    def flat(rows):
        return rows.reshape(-1, rows.shape[-1])

    def both_right(rows):
        rows = flat(rows)
        return jnp.concatenate([rows, lax.ppermute(rows, "rep", swap)], axis=0)

    def both_left(rows):
        rows = flat(rows)
        tokens, width = rows.shape
        half = width // (2 * GRID)
        cut = rows.T.reshape(GRID, 2, half, tokens)
        front = cut[:, 0].reshape(width // 2, tokens)
        back = cut[:, 1].reshape(width // 2, tokens)
        keep = jnp.where(core == 0, front, back)
        give = jnp.where(core == 0, back, front)
        both = jnp.concatenate([keep, lax.ppermute(give, "rep", swap)], axis=1)
        return both.reshape(NZ, NY, NX, half, 2 * tokens)

    normed, grad_proj = both_left(pairs[0][0]), both_right(pairs[0][1])
    mixed_low, grad_res_low = both_left(pairs[1][0]), both_right(pairs[1][1])
    grad_qkv = both_right(pairs[2][1])
    attended = both_left(pairs[3][0])
    normed_two, grad_gu = both_left(pairs[4][0]), both_right(pairs[4][1])
    activated, cotangent = both_left(pairs[5][0]), both_right(pairs[5][1])
    grad_gain_one, grad_conv_weight, grad_conv_bias, grad_gain_mix, grad_gain_two, grad_head = (
        smalls
    )
    packet = pack_small(
        [
            grad_gain_one.reshape(GRID, d_loc),
            grad_conv_weight.reshape(CONV, GRID, c_loc).transpose(1, 0, 2).reshape(GRID, -1),
            grad_conv_bias.reshape(GRID, c_loc),
            grad_gain_mix.reshape(GRID, m_loc),
            grad_gain_two.reshape(GRID, d_loc),
        ]
    )
    head_row = jnp.pad(grad_head.reshape(1, -1), ((0, 0), (0, 1024 - 3 * HEADS)))
    own_small = jnp.concatenate(
        [packet[:, :1024].reshape(GRID * 8, 128), head_row.reshape(8, 128)], axis=0
    )
    chip_small = own_small + lax.ppermute(own_small, "rep", swap)
    small_part = chip_small[: GRID * 8].reshape(GRID, 8, 128)
    small_part = jnp.where(core == 0, small_part, 0.0).reshape(NZ, NY, NX, 8, 128)
    head_sum, sums = scatter_all(
        chip_small[GRID * 8 :],
        small_part,
        [normed, mixed_low, normed_two, activated, attended],
        [grad_qkv, grad_proj, grad_res_low, grad_gu, cotangent],
        ((0, 0), (0, 1), (1, 2), (2, 3), (3, 4), (4, 2)),
    )
    row = sums[0].reshape(2, 1024)[0]
    cuts = [row[marks[k] : marks[k + 1]] for k in range(5)]
    return (
        hidden_out,
        input_grad,
        cuts[0],
        sums[2],
        cuts[1].reshape(CONV, c_loc),
        cuts[2],
        head_sum.reshape(-1)[: 3 * HEADS].reshape(3, HEADS),
        cuts[3],
        sums[3],
        sums[1],
        sums[6],
        cuts[4],
        sums[4],
        sums[5],
    )


def solution(mesh):
    grid = mesh.shape["fsdp"] == GRID and mesh.shape["rep"] == 2
    return jax.shard_map(
        on_device_grid if grid else on_device_any,
        mesh=mesh,
        in_specs=(
            P(None, ("fsdp", "rep"), None),
            P(None, ("fsdp", "rep"), None),
            P(None, ("fsdp", "rep"), None),
            P("fsdp"),
            P("fsdp", None),
            P(None, "fsdp"),
            P("fsdp"),
            P(),
            P("fsdp"),
            P("fsdp", None),
            P("fsdp", None),
            P("fsdp", None),
            P("fsdp"),
            P("fsdp", None),
            P("fsdp", None),
        ),
        out_specs=(
            P(None, ("fsdp", "rep"), None),
            P(None, ("fsdp", "rep"), None),
            P("fsdp"),
            P("fsdp", None),
            P(None, "fsdp"),
            P("fsdp"),
            P(),
            P("fsdp"),
            P("fsdp", None),
            P("fsdp", None),
            P("fsdp", None),
            P("fsdp"),
            P("fsdp", None),
            P("fsdp", None),
        ),
        check_vma=False,
    )
```

```python
import functools
import math

import jax
import jax.numpy as jnp
from jax import lax
from jax.experimental import pallas as pl
from jax.experimental.pallas import tpu as pltpu
from jax.sharding import PartitionSpec as P

HEADS = 24
HEAD_DIM = 64
STATE = 128
CONV = 4
QUERY_HEADS = 8
KEY_VALUE_HEADS = 2
HEAD_SIZE = 64
FF = 2048
MICRO = 2
DSSM = 1536
XBC = 1792


epsilon = 1e-05
highest = lax.Precision.HIGHEST
rope_base = 10000.0


def dot_bf(left, right):
    return jnp.dot(left, right, preferred_element_type=jnp.float32)


def dot_left(left, right):
    return lax.dot_general(
        left, right, (((0,), (0,)), ((), ())), preferred_element_type=jnp.float32
    )


def dot_right(left, right):
    return lax.dot_general(
        left, right, (((1,), (1,)), ((), ())), preferred_element_type=jnp.float32
    )


def rms_scale(value_rows):
    return lax.rsqrt(jnp.mean(value_rows * value_rows, axis=1, keepdims=True) + epsilon)


def norm_back(grad_normed, value_rows, scale_rows, gain_row):
    weighted = grad_normed * gain_row[None, :]
    inner_mean = jnp.mean(weighted * value_rows, axis=1, keepdims=True)
    return scale_rows * weighted - value_rows * scale_rows * scale_rows * scale_rows * inner_mean


def silu_slope(value_rows):
    sigma_v = jax.nn.sigmoid(value_rows)
    return sigma_v * (1.0 + value_rows * (1.0 - sigma_v))


def layout(lengths, count_of_tokens):
    seq_ends = jnp.cumsum(lengths, dtype=jnp.int32)
    places = jnp.arange(count_of_tokens, dtype=jnp.int32)
    passed = (places[:, None] >= seq_ends[None, :]).astype(jnp.int32)
    segment = jnp.sum(passed, axis=1, dtype=jnp.int32)
    starts = jnp.sum(passed * lengths[None, :], axis=1, dtype=jnp.int32)
    return (segment, places - starts)


def delay_keep(segment, lag_rows):
    count_of_tokens = segment.shape[0]
    earlier = jnp.concatenate(
        [jnp.full((lag_rows,), -1, jnp.int32), segment[: count_of_tokens - lag_rows]], axis=0
    )
    return earlier == segment


def delayed(value_rows, segment, lag_rows):
    count_of_tokens = value_rows.shape[0]
    shifted = jnp.concatenate(
        [
            jnp.zeros((lag_rows, value_rows.shape[1]), value_rows.dtype),
            value_rows[: count_of_tokens - lag_rows],
        ],
        axis=0,
    )
    return jnp.where(delay_keep(segment, lag_rows)[:, None], shifted, 0.0)


def rotary(position):
    half_width = HEAD_SIZE // 2
    inverse_freq = jnp.exp(
        jnp.arange(half_width, dtype=jnp.float32) * (-2.0 * math.log(rope_base) / HEAD_SIZE)
    )
    angles = position.astype(jnp.float32)[:, None] * inverse_freq[None, :]
    cosine_table = jnp.concatenate([jnp.cos(angles), jnp.cos(angles)], axis=1)
    sine_table = jnp.concatenate([jnp.sin(angles), jnp.sin(angles)], axis=1)
    return (cosine_table, sine_table)


def rotate(value_rows):
    first_half, second_half = jnp.split(value_rows, 2, axis=-1)
    return jnp.concatenate([-second_half, first_half], axis=-1)


def rotate_back(value_rows):
    first_half, second_half = jnp.split(value_rows, 2, axis=-1)
    return jnp.concatenate([second_half, -first_half], axis=-1)


def collect(
    in_gain,
    mixer_in,
    conv_weight,
    conv_bias,
    mixer_gain,
    mixer_out,
    qkv_weight,
    attn_out,
    ffn_gain,
    gate_up,
    ffn_down,
):
    return (
        lax.all_gather(in_gain, "fsdp", axis=0, tiled=True),
        lax.all_gather(mixer_in, "fsdp", axis=0, tiled=True),
        lax.all_gather(conv_weight, "fsdp", axis=1, tiled=True),
        lax.all_gather(conv_bias, "fsdp", axis=0, tiled=True),
        lax.all_gather(mixer_gain, "fsdp", axis=0, tiled=True),
        lax.all_gather(mixer_out, "fsdp", axis=0, tiled=True),
        lax.all_gather(qkv_weight, "fsdp", axis=0, tiled=True),
        lax.all_gather(attn_out, "fsdp", axis=0, tiled=True),
        lax.all_gather(ffn_gain, "fsdp", axis=0, tiled=True),
        lax.all_gather(gate_up, "fsdp", axis=0, tiled=True),
        lax.all_gather(ffn_down, "fsdp", axis=0, tiled=True),
    )


def micro_step(tokens, lengths, cotangent, gathered, head_params):
    (
        in_gain,
        mixer_in,
        conv_weight,
        conv_bias,
        mixer_gain,
        mixer_out,
        qkv_weight,
        attn_out,
        ffn_gain,
        gate_up,
        ffn_down,
    ) = gathered
    count_of_tokens = tokens.shape[0]
    x_float = tokens.astype(jnp.float32)
    segment, position = layout(lengths, count_of_tokens)
    places = jnp.arange(count_of_tokens, dtype=jnp.int32)
    visible = (segment[:, None] == segment[None, :]) & (places[:, None] >= places[None, :])
    gain_one = in_gain.astype(jnp.float32)
    scale_one = rms_scale(x_float)
    normed = (x_float * scale_one * gain_one[None, :]).astype(jnp.bfloat16)
    projected = dot_bf(normed, mixer_in)
    gate_z = projected[:, :DSSM]
    conv_input = projected[:, DSSM : DSSM + XBC]
    step_raw = projected[:, DSSM + XBC :]
    conv_taps = conv_weight.astype(jnp.float32)
    conv_sum = jnp.broadcast_to(conv_bias.astype(jnp.float32)[None, :], (count_of_tokens, XBC))
    tap_inputs = []
    for offset in range(CONV):
        tap_value = delayed(conv_input, segment, CONV - 1 - offset)
        tap_inputs.append(tap_value)
        conv_sum = conv_sum + conv_taps[offset][None, :] * tap_value
    conv_out = jax.nn.silu(conv_sum)
    inner_x = conv_out[:, :DSSM].reshape(count_of_tokens, HEADS, HEAD_DIM)
    input_b = conv_out[:, DSSM : DSSM + STATE]
    input_c = conv_out[:, DSSM + STATE :]
    step_in = step_raw + head_params[0][None, :]
    step_size = jax.nn.softplus(step_in)
    decay_rate = -jnp.exp(head_params[1])
    skip_factor = head_params[2]
    cumulative = jnp.cumsum(step_size * decay_rate[None, :], axis=0)
    inside = visible[:, :, None]
    decay_mask = jnp.where(
        inside,
        jnp.exp(jnp.where(inside, cumulative[:, None, :] - cumulative[None, :, :], 0.0)),
        0.0,
    )
    intersection = jnp.dot(input_c, input_b.T, precision=highest)
    mixing = intersection[:, :, None] * decay_mask
    scaled_in = inner_x * step_size[:, :, None]
    ssd_out = (
        jnp.einsum("tsh,shp->thp", mixing, scaled_in, precision=highest)
        + skip_factor[None, :, None] * inner_x
    )
    flat_ssd = ssd_out.reshape(count_of_tokens, DSSM)
    silu_z = jax.nn.silu(gate_z)
    gated_out = flat_ssd * silu_z
    gain_mix = mixer_gain.astype(jnp.float32)
    scale_two = rms_scale(gated_out)
    mixed_low = (gated_out * scale_two * gain_mix[None, :]).astype(jnp.bfloat16)
    mixer_branch = dot_bf(mixed_low, mixer_out)
    query_key_value_output = dot_bf(normed, qkv_weight)
    query_group_width = QUERY_HEADS // KEY_VALUE_HEADS
    query_rows = query_key_value_output[:, : QUERY_HEADS * HEAD_SIZE].reshape(
        count_of_tokens, KEY_VALUE_HEADS, query_group_width, HEAD_SIZE
    )
    key_matrix_rows = query_key_value_output[
        :, QUERY_HEADS * HEAD_SIZE : (QUERY_HEADS + KEY_VALUE_HEADS) * HEAD_SIZE
    ].reshape(count_of_tokens, KEY_VALUE_HEADS, HEAD_SIZE)
    value_rows = query_key_value_output[:, (QUERY_HEADS + KEY_VALUE_HEADS) * HEAD_SIZE :].reshape(
        count_of_tokens, KEY_VALUE_HEADS, HEAD_SIZE
    )
    cosine_table, sine_table = rotary(position)
    rot_q = (
        query_rows * cosine_table[:, None, None, :]
        + rotate(query_rows) * sine_table[:, None, None, :]
    ).astype(jnp.bfloat16)
    rot_k = (
        key_matrix_rows * cosine_table[:, None, :]
        + rotate(key_matrix_rows) * sine_table[:, None, :]
    ).astype(jnp.bfloat16)
    value_low = value_rows.astype(jnp.bfloat16)
    score_scale = HEAD_SIZE ** (-0.5)
    scores = (
        jnp.einsum("tkgd,skd->kgts", rot_q, rot_k, preferred_element_type=jnp.float32) * score_scale
    )
    scores = jnp.where(visible[None, None], scores, -1e30)
    exponent = jnp.exp(scores - jnp.max(scores, axis=3, keepdims=True))
    attention_probs = exponent / jnp.sum(exponent, axis=3, keepdims=True)
    probs_low = attention_probs.astype(jnp.bfloat16)
    attended = jnp.einsum(
        "kgts,skd->tkgd", probs_low, value_low, preferred_element_type=jnp.float32
    )
    attended = attended.reshape(count_of_tokens, QUERY_HEADS * HEAD_SIZE).astype(jnp.bfloat16)
    attn_branch = dot_bf(attended, attn_out)
    residual = x_float + mixer_branch + attn_branch
    gain_two = ffn_gain.astype(jnp.float32)
    scale_three = rms_scale(residual)
    normed_two = (residual * scale_three * gain_two[None, :]).astype(jnp.bfloat16)
    gate_upv = dot_bf(normed_two, gate_up)
    gate_part = gate_upv[:, :FF]
    up_part = gate_upv[:, FF:]
    activated = (jax.nn.silu(gate_part) * up_part).astype(jnp.bfloat16)
    ffn_branch = dot_bf(activated, ffn_down)
    output = (residual + ffn_branch).astype(jnp.bfloat16)
    grad_out = cotangent.astype(jnp.float32)
    grad_act = dot_right(cotangent, ffn_down)
    grad_gu = jnp.concatenate(
        [grad_act * up_part * silu_slope(gate_part), grad_act * jax.nn.silu(gate_part)], axis=1
    ).astype(jnp.bfloat16)
    grad_n_two = dot_right(grad_gu, gate_up)
    grad_gain_two = jnp.sum(grad_n_two * residual * scale_three, axis=0)
    grad_residual = grad_out + norm_back(grad_n_two, residual, scale_three, gain_two)
    grad_res_low = grad_residual.astype(jnp.bfloat16)
    grad_att = (
        dot_right(grad_res_low, attn_out)
        .astype(jnp.bfloat16)
        .reshape(count_of_tokens, KEY_VALUE_HEADS, query_group_width, HEAD_SIZE)
    )
    value_gradient = jnp.einsum(
        "kgts,tkgd->skd", probs_low, grad_att, preferred_element_type=jnp.float32
    )
    grad_probs = jnp.einsum(
        "tkgd,skd->kgts", grad_att, value_low, preferred_element_type=jnp.float32
    )
    grad_scores = attention_probs * (
        grad_probs - jnp.sum(grad_probs * attention_probs, axis=3, keepdims=True)
    )
    grad_scores_low = grad_scores.astype(jnp.bfloat16)
    grad_rot_q = (
        jnp.einsum("kgts,skd->tkgd", grad_scores_low, rot_k, preferred_element_type=jnp.float32)
        * score_scale
    )
    grad_rot_k = (
        jnp.einsum("kgts,tkgd->skd", grad_scores_low, rot_q, preferred_element_type=jnp.float32)
        * score_scale
    )
    grad_q = grad_rot_q * cosine_table[:, None, None, :] + rotate_back(
        grad_rot_q * sine_table[:, None, None, :]
    )
    key_gradient = grad_rot_k * cosine_table[:, None, :] + rotate_back(
        grad_rot_k * sine_table[:, None, :]
    )
    grad_qkv = jnp.concatenate(
        [
            grad_q.reshape(count_of_tokens, QUERY_HEADS * HEAD_SIZE),
            key_gradient.reshape(count_of_tokens, KEY_VALUE_HEADS * HEAD_SIZE),
            value_gradient.reshape(count_of_tokens, KEY_VALUE_HEADS * HEAD_SIZE),
        ],
        axis=1,
    ).astype(jnp.bfloat16)
    grad_mixed = dot_right(grad_res_low, mixer_out)
    grad_gain_mix = jnp.sum(grad_mixed * gated_out * scale_two, axis=0)
    grad_gated = norm_back(grad_mixed, gated_out, scale_two, gain_mix)
    grad_ssd = (grad_gated * silu_z).reshape(count_of_tokens, HEADS, HEAD_DIM)
    grad_z = grad_gated * flat_ssd * silu_slope(gate_z)
    grad_skip = jnp.sum(grad_ssd * inner_x, axis=(0, 2))
    grad_scaled = jnp.einsum("tsh,thp->shp", mixing, grad_ssd, precision=highest)
    grad_mixing = jnp.einsum("thp,shp->tsh", grad_ssd, scaled_in, precision=highest)
    grad_intersection = jnp.sum(grad_mixing * decay_mask, axis=2)
    grad_differ = grad_mixing * mixing
    grad_cumul = jnp.sum(grad_differ, axis=1) - jnp.sum(grad_differ, axis=0)
    grad_logs = jnp.cumsum(grad_cumul[::-1], axis=0)[::-1]
    grad_delta = grad_logs * decay_rate[None, :] + jnp.sum(grad_scaled * inner_x, axis=2)
    grad_rate_log = jnp.sum(grad_logs * step_size, axis=0) * decay_rate
    grad_inner = grad_scaled * step_size[:, :, None] + skip_factor[None, :, None] * grad_ssd
    grad_step = grad_delta * jax.nn.sigmoid(step_in)
    grad_head = jnp.stack([jnp.sum(grad_step, axis=0), grad_rate_log, grad_skip], axis=0)
    grad_c = jnp.dot(grad_intersection, input_b, precision=highest)
    grad_b = jnp.dot(grad_intersection.T, input_c, precision=highest)
    grad_conv_out = jnp.concatenate(
        [grad_inner.reshape(count_of_tokens, DSSM), grad_b, grad_c], axis=1
    )
    grad_conv_sum = grad_conv_out * silu_slope(conv_sum)
    grad_conv_bias = jnp.sum(grad_conv_sum, axis=0)
    grad_conv_weight = jnp.stack(
        [jnp.sum(grad_conv_sum * tap_inputs[offset], axis=0) for offset in range(CONV)], axis=0
    )
    grad_conv_in = jnp.zeros((count_of_tokens, XBC), jnp.float32)
    for offset in range(CONV):
        lag_rows = CONV - 1 - offset
        tap_term = jnp.where(
            delay_keep(segment, lag_rows)[:, None], grad_conv_sum * conv_taps[offset][None, :], 0.0
        )
        grad_conv_in = grad_conv_in + jnp.concatenate(
            [tap_term[lag_rows:], jnp.zeros((lag_rows, XBC), jnp.float32)], axis=0
        )
    grad_proj = jnp.concatenate([grad_z, grad_conv_in, grad_step], axis=1).astype(jnp.bfloat16)
    grad_normed = dot_right(grad_proj, mixer_in) + dot_right(grad_qkv, qkv_weight)
    grad_gain_one = jnp.sum(grad_normed * x_float * scale_one, axis=0)
    grad_input = grad_residual + norm_back(grad_normed, x_float, scale_one, gain_one)
    pairs = (
        (normed, grad_proj),
        (mixed_low, grad_res_low),
        (normed, grad_qkv),
        (attended, grad_res_low),
        (normed_two, grad_gu),
        (activated, cotangent),
    )
    smalls = (
        grad_gain_one,
        grad_conv_weight,
        grad_conv_bias,
        grad_gain_mix,
        grad_gain_two,
        grad_head,
    )
    return (output, grad_input, pairs, smalls)


def on_device_any(
    hidden_in,
    seq_lengths,
    out_grad,
    in_gain,
    mixer_in,
    conv_weight,
    conv_bias,
    head_params,
    mixer_gain,
    mixer_out,
    qkv_weight,
    attn_out,
    ffn_gain,
    gate_up,
    ffn_down,
):
    gathered = None
    gathered = collect(
        in_gain,
        mixer_in,
        conv_weight,
        conv_bias,
        mixer_gain,
        mixer_out,
        qkv_weight,
        attn_out,
        ffn_gain,
        gate_up,
        ffn_down,
    )
    outputs = []
    input_grads = []
    kept_rows = []
    small_total = None
    for micro_index in range(MICRO):
        output, grad_input, pairs, smalls = micro_step(
            hidden_in[micro_index],
            seq_lengths[micro_index, 0],
            out_grad[micro_index],
            gathered,
            head_params,
        )
        outputs.append(output)
        input_grads.append(grad_input)
        kept_rows.append(pairs)
        small_total = smalls if small_total is None else jax.tree.map(jnp.add, small_total, smalls)
    full_grads = []
    for pair_index in range(6):
        left_rows = jnp.concatenate(
            [kept_rows[micro_index][pair_index][0] for micro_index in range(MICRO)], axis=0
        )
        right_rows = jnp.concatenate(
            [kept_rows[micro_index][pair_index][1] for micro_index in range(MICRO)], axis=0
        )
        full_grads.append(dot_left(left_rows, right_rows))
    grad_gain_one, grad_conv_weight, grad_conv_bias, grad_gain_mix, grad_gain_two, grad_head = (
        small_total
    )
    grad_terms = (
        grad_gain_one,
        full_grads[0],
        grad_conv_weight,
        grad_conv_bias,
        grad_gain_mix,
        full_grads[1],
        full_grads[2],
        full_grads[3],
        grad_gain_two,
        full_grads[4],
        full_grads[5],
    )
    shard_grads = (
        lax.psum_scatter(grad_terms[0], "fsdp", scatter_dimension=0, tiled=True),
        lax.psum_scatter(grad_terms[1], "fsdp", scatter_dimension=0, tiled=True),
        lax.psum_scatter(grad_terms[2], "fsdp", scatter_dimension=1, tiled=True),
        lax.psum_scatter(grad_terms[3], "fsdp", scatter_dimension=0, tiled=True),
        lax.psum_scatter(grad_terms[4], "fsdp", scatter_dimension=0, tiled=True),
        lax.psum_scatter(grad_terms[5], "fsdp", scatter_dimension=0, tiled=True),
        lax.psum_scatter(grad_terms[6], "fsdp", scatter_dimension=0, tiled=True),
        lax.psum_scatter(grad_terms[7], "fsdp", scatter_dimension=0, tiled=True),
        lax.psum_scatter(grad_terms[8], "fsdp", scatter_dimension=0, tiled=True),
        lax.psum_scatter(grad_terms[9], "fsdp", scatter_dimension=0, tiled=True),
        lax.psum_scatter(grad_terms[10], "fsdp", scatter_dimension=0, tiled=True),
    )
    halves = (
        lax.psum_scatter(
            shard_grads[0].astype(jnp.bfloat16), "rep", scatter_dimension=0, tiled=True
        ).astype(jnp.float32),
        lax.psum_scatter(
            shard_grads[1].astype(jnp.bfloat16), "rep", scatter_dimension=0, tiled=True
        ).astype(jnp.float32),
        lax.psum_scatter(
            shard_grads[2].astype(jnp.bfloat16), "rep", scatter_dimension=1, tiled=True
        ).astype(jnp.float32),
        lax.psum_scatter(
            shard_grads[3].astype(jnp.bfloat16), "rep", scatter_dimension=0, tiled=True
        ).astype(jnp.float32),
        lax.psum_scatter(
            shard_grads[4].astype(jnp.bfloat16), "rep", scatter_dimension=0, tiled=True
        ).astype(jnp.float32),
        lax.psum_scatter(
            shard_grads[5].astype(jnp.bfloat16), "rep", scatter_dimension=0, tiled=True
        ).astype(jnp.float32),
        lax.psum_scatter(
            shard_grads[6].astype(jnp.bfloat16), "rep", scatter_dimension=0, tiled=True
        ).astype(jnp.float32),
        lax.psum_scatter(
            shard_grads[7].astype(jnp.bfloat16), "rep", scatter_dimension=0, tiled=True
        ).astype(jnp.float32),
        lax.psum_scatter(
            shard_grads[8].astype(jnp.bfloat16), "rep", scatter_dimension=0, tiled=True
        ).astype(jnp.float32),
        lax.psum_scatter(
            shard_grads[9].astype(jnp.bfloat16), "rep", scatter_dimension=0, tiled=True
        ).astype(jnp.float32),
        lax.psum_scatter(
            shard_grads[10].astype(jnp.bfloat16), "rep", scatter_dimension=0, tiled=True
        ).astype(jnp.float32),
    )
    head_total = lax.psum(grad_head, ("fsdp", "rep"))
    summed = (
        lax.all_gather(halves[0].astype(jnp.bfloat16), "rep", axis=0, tiled=True).astype(
            jnp.float32
        ),
        lax.all_gather(halves[1].astype(jnp.bfloat16), "rep", axis=0, tiled=True).astype(
            jnp.float32
        ),
        lax.all_gather(halves[2].astype(jnp.bfloat16), "rep", axis=1, tiled=True).astype(
            jnp.float32
        ),
        lax.all_gather(halves[3].astype(jnp.bfloat16), "rep", axis=0, tiled=True).astype(
            jnp.float32
        ),
        lax.all_gather(halves[4].astype(jnp.bfloat16), "rep", axis=0, tiled=True).astype(
            jnp.float32
        ),
        lax.all_gather(halves[5].astype(jnp.bfloat16), "rep", axis=0, tiled=True).astype(
            jnp.float32
        ),
        lax.all_gather(halves[6].astype(jnp.bfloat16), "rep", axis=0, tiled=True).astype(
            jnp.float32
        ),
        lax.all_gather(halves[7].astype(jnp.bfloat16), "rep", axis=0, tiled=True).astype(
            jnp.float32
        ),
        lax.all_gather(halves[8].astype(jnp.bfloat16), "rep", axis=0, tiled=True).astype(
            jnp.float32
        ),
        lax.all_gather(halves[9].astype(jnp.bfloat16), "rep", axis=0, tiled=True).astype(
            jnp.float32
        ),
        lax.all_gather(halves[10].astype(jnp.bfloat16), "rep", axis=0, tiled=True).astype(
            jnp.float32
        ),
    )
    hidden_out = jnp.stack(outputs, axis=0)
    input_grad = jnp.stack(input_grads, axis=0)
    return (
        hidden_out,
        input_grad,
        summed[0],
        summed[1],
        summed[2],
        summed[3],
        head_total,
        summed[4],
        summed[5],
        summed[6],
        summed[7],
        summed[8],
        summed[9],
        summed[10],
    )


MESH = pl.DeviceIdType.MESH
NZ, NY, NX = 4, 2, 2
GRID = NZ * NY * NX


def positions():
    chip = lax.axis_index("fsdp")
    core = lax.axis_index("rep")
    z = chip // (NY * NX)
    y = (chip // NX) % NY
    x = chip % NX
    y1 = (y + core) % 2
    x1 = (x + 1 - core) % 2
    y2 = (y + 1 - core) % 2
    x2 = (x + core) % 2
    return z, y, x, y1, x1, y2, x2, core


def chip_of(z, y, x):
    return (z * NY + y) * NX + x


def greet(z, y, x, y1, x1, y2, x2, core):
    barrier = pltpu.get_barrier_semaphore()
    partners = [(chip_of((z + dz) % NZ, y, x), core) for dz in range(1, NZ)]
    partners += [(chip_of(z, y1, x1), core), (chip_of(z, y2, x2), core)]
    partners += [(chip_of(z, y, x), 1 - core)]
    for partner in partners:
        pl.semaphore_signal(barrier, inc=1, device_id=partner, device_id_type=MESH)
    pl.semaphore_wait(barrier, len(partners))


def push(src_ref, dst_ref, send_sem, recv_sem, partner):
    return pltpu.make_async_remote_copy(
        src_ref=src_ref,
        dst_ref=dst_ref,
        send_sem=send_sem,
        recv_sem=recv_sem,
        device_id=partner,
        device_id_type=MESH,
    )


def gather_kernel(count, *refs):
    shards = refs[:count]
    wholes = refs[count : 2 * count]
    own_sem, send_sem, recv_sem = refs[2 * count :]
    z, y, x, y1, x1, y2, x2, core = positions()
    greet(z, y, x, y1, x1, y2, x2, core)
    to_first = (chip_of(z, y1, x1), core)
    to_second = (chip_of(z, y2, x2), core)
    to_other = (chip_of(z, y, x), 1 - core)
    plan = []
    for w in range(count):
        half = shards[w].shape[0] // 2
        rows = pl.ds(pl.multiple_of(core * half, half), half)
        whole = wholes[w]
        own = pltpu.make_async_copy(shards[w].at[rows], whole.at[z, y, x, rows], own_sem.at[w])
        along_z = [
            push(
                shards[w].at[rows],
                whole.at[z, y, x, rows],
                send_sem.at[w, dz - 1],
                recv_sem.at[w, dz - 1],
                (chip_of((z + dz) % NZ, y, x), core),
            )
            for dz in range(1, NZ)
        ]
        column = whole.at[:, y, x, rows]
        column_first = whole.at[:, y1, x1, rows]
        along_first = push(column, column, send_sem.at[w, 3], recv_sem.at[w, 3], to_first)
        second_a = push(column, column, send_sem.at[w, 4], recv_sem.at[w, 4], to_second)
        second_b = push(column_first, column_first, send_sem.at[w, 5], recv_sem.at[w, 5], to_second)
        half_all = whole.at[:, :, :, rows]
        across = push(half_all, half_all, send_sem.at[w, 6], recv_sem.at[w, 6], to_other)
        plan.append((own, along_z, along_first, second_a, second_b, across))
    for own, along_z, _, _, _, _ in plan:
        own.start()
        for copy in along_z:
            copy.start()
    for step in range(count + 2):
        if step < count:
            own, along_z, along_first, second_a, _, _ = plan[step]
            own.wait()
            for copy in along_z:
                copy.wait_recv()
            along_first.start()
            second_a.start()
        if 1 <= step <= count:
            _, _, along_first, _, second_b, _ = plan[step - 1]
            along_first.wait_recv()
            second_b.start()
        if step >= 2:
            _, _, _, second_a, second_b, across = plan[step - 2]
            second_a.wait_recv()
            second_b.wait_recv()
            across.start()
    for _, along_z, along_first, second_a, second_b, across in plan:
        for copy in along_z:
            copy.wait_send()
        along_first.wait_send()
        second_a.wait_send()
        second_b.wait_send()
        across.wait()


def gather_all(shards):
    count = len(shards)
    gathered = pl.pallas_call(
        functools.partial(gather_kernel, count),
        out_shape=[
            jax.ShapeDtypeStruct((NZ, NY, NX) + shard.shape, shard.dtype) for shard in shards
        ],
        in_specs=[pl.BlockSpec(memory_space=pl.ANY)] * count,
        out_specs=[pl.BlockSpec(memory_space=pl.ANY)] * count,
        scratch_shapes=[
            pltpu.SemaphoreType.DMA((count,)),
            pltpu.SemaphoreType.DMA((count, 7)),
            pltpu.SemaphoreType.DMA((count, 7)),
        ],
        compiler_params=pltpu.CompilerParams(collective_id=0, has_side_effects=True),
        name="gather_weights",
    )(*shards)
    return [
        whole.reshape((GRID * shard.shape[0],) + shard.shape[1:])
        for whole, shard in zip(gathered, shards)
    ]


CHUNK = 512


def scatter_kernel(pick, *refs):
    count = 1 + len(pick)
    lefts = 1 + max(left for left, _ in pick)
    rights = 1 + max(right for _, right in pick)
    head_ref, small_ref = refs[:2]
    keep_refs = refs[2 : 2 + lefts]
    give_refs = refs[2 + lefts : 2 + 2 * lefts]
    own_refs = refs[2 + 2 * lefts : 2 + 2 * lefts + rights]
    refs = refs[2 + 2 * lefts + rights :]
    head_out = refs[0]
    outs = refs[1 : 1 + count]
    rest = refs[1 + count :]
    grads = rest[:count]
    got_second = rest[count : 2 * count]
    got_first = rest[2 * count : 3 * count]
    got_z = rest[3 * count : 4 * count]
    total = rest[4 * count : 5 * count]
    heads, store_sem, send_sem, recv_sem, head_send, head_recv = rest[5 * count : 5 * count + 6]
    rest = rest[5 * count + 6 :]
    left_refs = rest[:lefts]
    right_refs = rest[lefts : lefts + rights]
    keep_sem, swap_send, swap_recv = rest[lefts + rights :]
    z, y, x, y1, x1, y2, x2, core = positions()
    targets = ((1 - y, 1 - x), (y2, x2), (y1, x1), (y, x))
    greet(z, y, x, y1, x1, y2, x2, core)
    to_first = (chip_of(z, y1, x1), core)
    to_second = (chip_of(z, y2, x2), core)
    to_other = (chip_of(z, y, x), 1 - core)
    z_peers = [((z + dz) % NZ, (chip_of((z + dz) % NZ, y, x), core)) for dz in range(1, NZ)]
    f32 = jnp.float32

    head_z = [
        push(head_ref, heads.at[z, y, x], head_send.at[k], head_recv.at[k], z_peers[k][1])
        for k in range(NZ - 1)
    ]
    for copy in head_z:
        copy.start()
    heads[z, y, x] = head_ref[...]

    swaps = {}
    for left, right in pick:
        for name, at in (("l", left), ("r", right)):
            if (name, at) in swaps:
                continue
            k = len(swaps)
            if name == "l":
                tokens = keep_refs[at].shape[4]
                span = pl.ds(pl.multiple_of(core * tokens, tokens), tokens)
                mine, sent = keep_refs[at], give_refs[at]
                spot = left_refs[at].at[:, :, :, :, span]
            else:
                tokens = own_refs[at].shape[0]
                span = pl.ds(pl.multiple_of(core * tokens, tokens), tokens)
                mine, sent = own_refs[at], own_refs[at]
                spot = right_refs[at].at[span]
            kept = pltpu.make_async_copy(mine, spot, keep_sem.at[k])
            moved = push(sent, spot, swap_send.at[k], swap_recv.at[k], to_other)
            swaps[(name, at)] = (kept, moved)
            moved.start()
            kept.start()
    ready = set()

    def need(key):
        if key not in ready:
            ready.add(key)
            swaps[key][0].wait()
            swaps[key][1].wait_recv()

    def fill(w, place):
        row, column = targets[place]
        if w == 0:
            grads[0][place] = small_ref[:, row, column]
            return
        need(("l", pick[w - 1][0]))
        need(("r", pick[w - 1][1]))
        left_ref = left_refs[pick[w - 1][0]]
        right_ref = right_refs[pick[w - 1][1]]
        left = jnp.concatenate([left_ref[k, row, column] for k in range(NZ)], axis=0)
        width = right_ref.shape[1]
        half = left_ref.shape[3]

        def some(columns, size):
            block = jnp.dot(left, right_ref[:, columns], preferred_element_type=f32)
            block = block.astype(jnp.bfloat16)
            grads[w][place, :, :, columns] = block.reshape(NZ, half, size)

        @pl.loop(0, width // CHUNK)
        def _(step):
            some(pl.ds(pl.multiple_of(step * CHUNK, CHUNK), CHUNK), CHUNK)

        if width % CHUNK:
            some(pl.ds(width // CHUNK * CHUNK, width % CHUNK), width % CHUNK)

    plan = []
    for w in range(count):
        far = [
            push(
                grads[w].at[k],
                got_second[w].at[k],
                send_sem.at[w, k],
                recv_sem.at[w, k],
                to_second,
            )
            for k in range(2)
        ]
        near = push(grads[w].at[2], got_first[w], send_sem.at[w, 2], recv_sem.at[w, 2], to_first)
        along_z = [
            push(
                grads[w].at[3, z_peers[k][0]],
                got_z[w].at[k],
                send_sem.at[w, 3 + k],
                recv_sem.at[w, 3 + k],
                z_peers[k][1],
            )
            for k in range(NZ - 1)
        ]
        half = total[w].shape[0]
        rows = pl.ds(pl.multiple_of(core * half, half), half)
        across = push(total[w], outs[w].at[rows], send_sem.at[w, 6], recv_sem.at[w, 6], to_other)
        store = pltpu.make_async_copy(total[w], outs[w].at[rows], store_sem.at[w])
        plan.append((far, near, along_z, across, store))
        for k in range(2):
            fill(w, k)
            far[k].start()

    column = heads.at[:, y, x]
    column_first = heads.at[:, y1, x1]
    head_near = push(column, column, head_send.at[3], head_recv.at[3], to_first)
    head_far_a = push(column, column, head_send.at[4], head_recv.at[4], to_second)
    head_far_b = push(column_first, column_first, head_send.at[5], head_recv.at[5], to_second)
    for copy in head_z:
        copy.wait_recv()
    head_near.start()
    head_far_a.start()

    for w in range(count):
        fill(w, 2)
        fill(w, 3)

    head_near.wait_recv()
    head_far_b.start()

    for step in range(count + 2):
        if step < count:
            w = step
            far, near, _, _, _ = plan[w]
            far[0].wait_recv()

            @pl.loop(0, NZ)
            def _(k, w=w):
                mine = grads[w][2, k].astype(f32)
                grads[w][2, k] = (mine + got_second[w][0, k].astype(f32)).astype(grads[w].dtype)

            near.start()
        if 1 <= step <= count:
            w = step - 1
            far, near, along_z, _, _ = plan[w]
            far[1].wait_recv()
            near.wait_recv()

            @pl.loop(0, NZ)
            def _(k, w=w):
                mine = grads[w][3, k].astype(f32) + got_second[w][1, k].astype(f32)
                grads[w][3, k] = (mine + got_first[w][k].astype(f32)).astype(grads[w].dtype)

            for copy in along_z:
                copy.start()
        if step >= 2:
            w = step - 2
            _, _, along_z, across, store = plan[w]
            for copy in along_z:
                copy.wait_recv()
            result = grads[w][3, z].astype(f32)
            for k in range(NZ - 1):
                result = result + got_z[w][k].astype(f32)
            total[w][...] = result
            across.start()
            store.start()

    head_far_a.wait_recv()
    head_far_b.wait_recv()
    head_sum = heads[0, 0, 0]
    for k in range(1, GRID):
        head_sum = head_sum + heads[k // (NY * NX), (k // NX) % NY, k % NX]
    head_out[...] = head_sum
    for copy in head_z + [head_near, head_far_a, head_far_b]:
        copy.wait_send()
    for _, moved in swaps.values():
        moved.wait_send()
    for far, near, along_z, across, store in plan:
        for copy in far + [near] + along_z:
            copy.wait_send()
        across.wait()
        store.wait()


def scatter_all(head_part, small_part, keeps, gives, rights, pick):
    count = 1 + len(pick)
    units = [(small_part.shape[3:], small_part.dtype)]
    for left, right in pick:
        units.append(((keeps[left].shape[3], rights[right].shape[1]), jnp.bfloat16))
    scratch = [pltpu.VMEM((4, NZ) + shape, dtype) for shape, dtype in units]
    scratch += [pltpu.VMEM((2, NZ) + shape, dtype) for shape, dtype in units]
    scratch += [pltpu.VMEM((NZ,) + shape, dtype) for shape, dtype in units]
    scratch += [pltpu.VMEM((NZ - 1,) + shape, dtype) for shape, dtype in units]
    scratch += [pltpu.VMEM(shape, jnp.float32) for shape, dtype in units]
    scratch += [
        pltpu.VMEM((NZ, NY, NX) + head_part.shape, jnp.float32),
        pltpu.SemaphoreType.DMA((count,)),
        pltpu.SemaphoreType.DMA((count, 7)),
        pltpu.SemaphoreType.DMA((count, 7)),
        pltpu.SemaphoreType.DMA((6,)),
        pltpu.SemaphoreType.DMA((6,)),
    ]
    swapped = len(keeps) + len(rights)
    scratch += [
        pltpu.VMEM(keep.shape[:4] + (2 * keep.shape[4],), keep.dtype) for keep in keeps
    ]
    scratch += [
        pltpu.VMEM((2 * right.shape[0], right.shape[1]), right.dtype) for right in rights
    ]
    scratch += [pltpu.SemaphoreType.DMA((swapped,)) for _ in range(3)]
    operands = [head_part, small_part] + keeps + gives + rights
    result = pl.pallas_call(
        functools.partial(scatter_kernel, pick),
        out_shape=[jax.ShapeDtypeStruct(head_part.shape, jnp.float32)]
        + [
            jax.ShapeDtypeStruct((2 * shape[0],) + tuple(shape[1:]), jnp.float32)
            for shape, dtype in units
        ],
        in_specs=[pl.BlockSpec(memory_space=pltpu.VMEM)] * len(operands),
        out_specs=[pl.BlockSpec(memory_space=pltpu.VMEM)]
        + [pl.BlockSpec(memory_space=pl.ANY)] * count,
        scratch_shapes=scratch,
        compiler_params=pltpu.CompilerParams(
            collective_id=1, has_side_effects=True, vmem_limit_bytes=50 * 1024 * 1024
        ),
        name="scatter_gradients",
    )(*operands)
    return result[0], result[1:]


SMALL_ROWS = 32


def pack_small(pieces):
    rows = jnp.concatenate(pieces, axis=1)
    spare = SMALL_ROWS * 128 - rows.shape[1]
    return jnp.pad(rows, ((0, 0), (0, spare)))


def on_device_grid(
    hidden_in,
    seq_lengths,
    out_grad,
    in_gain,
    mixer_in,
    conv_weight,
    conv_bias,
    head_params,
    mixer_gain,
    mixer_out,
    qkv_weight,
    attn_out,
    ffn_gain,
    gate_up,
    ffn_down,
):
    small = pack_small(
        [
            in_gain[None],
            conv_weight.reshape(1, -1),
            conv_bias[None],
            mixer_gain[None],
            ffn_gain[None],
        ]
    ).reshape(SMALL_ROWS, 128)
    small_all, qkv_all, mixer_in_all, mixer_out_all, gate_up_all, ffn_down_all, attn_out_all = (
        gather_all([small, qkv_weight, mixer_in, mixer_out, gate_up, ffn_down, attn_out])
    )
    small_all = small_all.reshape(GRID, SMALL_ROWS * 128)
    d_loc, c_loc, m_loc = in_gain.shape[0], conv_bias.shape[0], mixer_gain.shape[0]
    marks = [0]
    for width in (d_loc, CONV * c_loc, c_loc, m_loc, d_loc):
        marks.append(marks[-1] + width)
    cuts = [small_all[:, marks[k] : marks[k + 1]] for k in range(5)]
    conv_all = cuts[1].reshape(GRID, CONV, c_loc).transpose(1, 0, 2).reshape(CONV, XBC)
    gathered = (
        cuts[0].reshape(-1),
        mixer_in_all,
        conv_all,
        cuts[2].reshape(-1),
        cuts[3].reshape(-1),
        mixer_out_all,
        qkv_all,
        attn_out_all,
        cuts[4].reshape(-1),
        gate_up_all,
        ffn_down_all,
    )
    hidden_out, input_grad, pairs, smalls = jax.vmap(
        lambda tokens, lengths, cotangent: micro_step(
            tokens, lengths, cotangent, gathered, head_params
        )
    )(hidden_in, seq_lengths[:, 0], out_grad)
    smalls = jax.tree.map(lambda value: jnp.sum(value, axis=0), smalls)
    core = lax.axis_index("rep")
    swap = [(0, 1), (1, 0)]

    def flat(rows):
        return rows.reshape(-1, rows.shape[-1])

    def halves_of(rows):
        rows = flat(rows)
        tokens, width = rows.shape
        half = width // (2 * GRID)
        cut = rows.T.reshape(NZ, NY, NX, 2, half, tokens)
        front, back = cut[:, :, :, 0], cut[:, :, :, 1]
        return jnp.where(core == 0, front, back), jnp.where(core == 0, back, front)

    keeps, gives = zip(*[halves_of(pairs[k][0]) for k in (0, 1, 4, 5, 3)])
    rights = [flat(pairs[k][1]) for k in (2, 0, 1, 4, 5)]
    grad_gain_one, grad_conv_weight, grad_conv_bias, grad_gain_mix, grad_gain_two, grad_head = (
        smalls
    )
    packet = pack_small(
        [
            grad_gain_one.reshape(GRID, d_loc),
            grad_conv_weight.reshape(CONV, GRID, c_loc).transpose(1, 0, 2).reshape(GRID, -1),
            grad_conv_bias.reshape(GRID, c_loc),
            grad_gain_mix.reshape(GRID, m_loc),
            grad_gain_two.reshape(GRID, d_loc),
        ]
    )
    head_row = jnp.pad(grad_head.reshape(1, -1), ((0, 0), (0, 1024 - 3 * HEADS)))
    own_small = jnp.concatenate(
        [packet[:, :1024].reshape(GRID * 8, 128), head_row.reshape(8, 128)], axis=0
    )
    chip_small = own_small + lax.ppermute(own_small, "rep", swap)
    small_part = chip_small[: GRID * 8].reshape(GRID, 8, 128)
    small_part = jnp.where(core == 0, small_part, 0.0).reshape(NZ, NY, NX, 8, 128)
    head_sum, sums = scatter_all(
        chip_small[GRID * 8 :],
        small_part,
        list(keeps),
        list(gives),
        rights,
        ((0, 0), (0, 1), (1, 2), (2, 3), (3, 4), (4, 2)),
    )
    row = sums[0].reshape(2, 1024)[0]
    cuts = [row[marks[k] : marks[k + 1]] for k in range(5)]
    return (
        hidden_out,
        input_grad,
        cuts[0],
        sums[2],
        cuts[1].reshape(CONV, c_loc),
        cuts[2],
        head_sum.reshape(-1)[: 3 * HEADS].reshape(3, HEADS),
        cuts[3],
        sums[3],
        sums[1],
        sums[6],
        cuts[4],
        sums[4],
        sums[5],
    )


def solution(mesh):
    grid = mesh.shape["fsdp"] == GRID and mesh.shape["rep"] == 2
    return jax.shard_map(
        on_device_grid if grid else on_device_any,
        mesh=mesh,
        in_specs=(
            P(None, ("fsdp", "rep"), None),
            P(None, ("fsdp", "rep"), None),
            P(None, ("fsdp", "rep"), None),
            P("fsdp"),
            P("fsdp", None),
            P(None, "fsdp"),
            P("fsdp"),
            P(),
            P("fsdp"),
            P("fsdp", None),
            P("fsdp", None),
            P("fsdp", None),
            P("fsdp"),
            P("fsdp", None),
            P("fsdp", None),
        ),
        out_specs=(
            P(None, ("fsdp", "rep"), None),
            P(None, ("fsdp", "rep"), None),
            P("fsdp"),
            P("fsdp", None),
            P(None, "fsdp"),
            P("fsdp"),
            P(),
            P("fsdp"),
            P("fsdp", None),
            P("fsdp", None),
            P("fsdp", None),
            P("fsdp"),
            P("fsdp", None),
            P("fsdp", None),
        ),
        check_vma=False,
    )
```
